32 devices in a mesh: dp: 16 (over z, y, core), shard: 2 (over x).
Axes of the slice: x: 2, y: 2, z: 4, core: 2. Of those that a mesh axis runs over, the one named last changes fastest.
Arguments:
- tokens: bfloat16 [32768, 768], P(('dp', 'shard')), may hold values from -6 to 6
- seq_lengths: int32 [32, 4], P(('dp', 'shard')), may hold values from 128 to 640, as said below
- query_weight: bfloat16 [768, 768], P(('dp', 'shard')), may hold values from -0.21875 to 0.21875
- query_bias: bfloat16 [768], P(('dp', 'shard')), may hold values from -3 to 3
- key_weight: bfloat16 [768, 768], P(('dp', 'shard')), may hold values from -0.21875 to 0.21875
- key_bias: bfloat16 [768], P(('dp', 'shard')), may hold values from -3 to 3
- value_weight: bfloat16 [768, 768], P(('dp', 'shard')), may hold values from -0.21875 to 0.21875
- value_bias: bfloat16 [768], P(('dp', 'shard')), may hold values from -3 to 3
- output_weight: bfloat16 [768, 768], P(('dp', 'shard')), may hold values from -0.875 to 0.875
- output_bias: bfloat16 [768], P(('dp', 'shard')), may hold values from -3 to 3
- norm_gain: bfloat16 [768], P(('dp', 'shard')), may hold values from 0.099609375 to 1.8984375
- norm_shift: bfloat16 [768], P(('dp', 'shard')), may hold values from -3 to 3
- inner_weight: bfloat16 [768, 3072], P(('dp', 'shard')), may hold values from -0.21875 to 0.21875
- inner_bias: bfloat16 [3072], P(('dp', 'shard')), may hold values from -3 to 3
- outer_weight: bfloat16 [3072, 768], P(('dp', 'shard')), may hold values from -0.109375 to 0.109375
- outer_bias: bfloat16 [768], P(('dp', 'shard')), may hold values from -3 to 3
- final_gain: bfloat16 [768], P(('dp', 'shard')), may hold values from 0.099609375 to 1.8984375
- final_shift: bfloat16 [768], P(('dp', 'shard')), may hold values from -3 to 3
- cotangent: bfloat16 [32768, 768], P(('dp', 'shard')), may hold values from -6 to 6
Outputs:
- layer_output: bfloat16 [32768, 768], P(('dp', 'shard'))
- tokens_grad: bfloat16 [32768, 768], P(('dp', 'shard'))
- query_weight_grad: float32 [768, 768], P(('dp', 'shard'))
- query_bias_grad: float32 [768], P(('dp', 'shard'))
- key_weight_grad: float32 [768, 768], P(('dp', 'shard'))
- key_bias_grad: float32 [768], P(('dp', 'shard'))
- value_weight_grad: float32 [768, 768], P(('dp', 'shard'))
- value_bias_grad: float32 [768], P(('dp', 'shard'))
- output_weight_grad: float32 [768, 768], P(('dp', 'shard'))
- output_bias_grad: float32 [768], P(('dp', 'shard'))
- norm_gain_grad: float32 [768], P(('dp', 'shard'))
- norm_shift_grad: float32 [768], P(('dp', 'shard'))
- inner_weight_grad: float32 [768, 3072], P(('dp', 'shard'))
- inner_bias_grad: float32 [3072], P(('dp', 'shard'))
- outer_weight_grad: float32 [3072, 768], P(('dp', 'shard'))
- outer_bias_grad: float32 [768], P(('dp', 'shard'))
- final_gain_grad: float32 [768], P(('dp', 'shard'))
- final_shift_grad: float32 [768], P(('dp', 'shard'))
The draws below stay inside these ranges and needn't reach their ends.
Inputs may be any that keep to these rules, and one draw needn't show every extreme that they name: `seq_lengths`: each device's 4 lengths sum to 1024; some device has one sequence of the largest length.
All inputs are finite; a program needn't handle non-finite values.
Results may differ from the reference program's by a relative error of at most 0.03.
Values may be sent and summed in bfloat16 or wider, within the bound.
A program may use at most 192 MiB of HBM per device.

```python
import math
import jax
import jax.numpy as jnp
from jax import lax

D = 768
HEADS = 12
HD = 64
FF = 3072
TOK_DEV = 1024
SEQ_DEV = 4
MIN_LEN = 128
TOKENS = 32768
DEVICES = 32


def draw_seq_lengths(key, part):
    key = jax.random.fold_in(key, 11)
    first_key, second_key, third_key = jax.random.split(key, 3)
    spare = TOK_DEV - SEQ_DEV * MIN_LEN
    cuts = jax.random.randint(first_key, (DEVICES, SEQ_DEV - 1), 0, spare + 1)
    cuts = jnp.sort(cuts, axis=1)
    edges = jnp.concatenate([jnp.zeros((DEVICES, 1), jnp.int32), cuts.astype(jnp.int32), jnp.full((DEVICES, 1), spare, jnp.int32)], axis=1)
    lengths = MIN_LEN + edges[:, 1:] - edges[:, :-1]
    picked = jax.random.randint(second_key, (), 0, DEVICES)
    longest = jax.random.randint(third_key, (), 0, SEQ_DEV)
    extreme = MIN_LEN + spare * (jnp.arange(SEQ_DEV) == longest).astype(jnp.int32)
    lengths = jnp.where((jnp.arange(DEVICES) == picked)[:, None], extreme[None, :], lengths)
    return lengths.astype(jnp.int32)


def levels(key, dims, pieces, smallest, high):
    level = 1.0
    for axis_at, shards_of in pieces:
        heights = jax.random.uniform(jax.random.fold_in(jax.random.fold_in(key, 6), axis_at), (shards_of,), jnp.float32, smallest / len(pieces), high / len(pieces))
        level = level * jnp.repeat(jnp.exp(heights), dims[axis_at] // shards_of).reshape((-1,) + (1,) * (len(dims) - 1 - axis_at))
    return level


def bell_draw(key, shape, scale, most, pieces=(), kind=jnp.bfloat16):
    loudness = levels(key, shape, pieces, -0.22, 0.18) if pieces else 1.0
    drawn = jax.random.normal(key, shape, jnp.float32) * scale * loudness
    return jnp.minimum(jnp.maximum(drawn, -most), most).astype(kind)


def setup_inputs(seed: int = 0) -> dict:
    key_list = jax.random.split(jax.random.key(seed), 20)
    tokens = bell_draw(key_list[0], (TOKENS, D), 1.0, 6.0, ((0, 32),))
    seq_lengths = draw_seq_lengths(jax.random.fold_in(key_list[19], 71), 0)
    query_weight = bell_draw(key_list[2], (D, D), D ** -0.5, 0.21875, ((0, 32),))
    query_bias = bell_draw(key_list[3], (D,), 0.5, 3.0, ((0, 32),))
    key_weight = bell_draw(key_list[4], (D, D), D ** -0.5, 0.21875, ((0, 32),))
    key_bias = bell_draw(key_list[5], (D,), 0.5, 3.0, ((0, 32),))
    value_weight = bell_draw(key_list[6], (D, D), D ** -0.5, 0.21875, ((0, 32),))
    value_bias = bell_draw(key_list[7], (D,), 0.5, 3.0, ((0, 32),))
    output_weight = bell_draw(key_list[8], (D, D), (D // 16) ** -0.5, 0.875, ((0, 32),))
    output_bias = bell_draw(key_list[9], (D,), 0.5, 3.0, ((0, 32),))
    norm_gain = jnp.clip(1.0 + 0.18 * jax.random.normal(key_list[10], (D,), jnp.float32), 0.099609375, 1.8984375).astype(jnp.bfloat16)
    norm_shift = bell_draw(key_list[11], (D,), 0.5, 3.0, ((0, 32),))
    inner_weight = bell_draw(key_list[12], (D, FF), D ** -0.5, 0.21875, ((0, 32),))
    inner_bias = bell_draw(key_list[13], (FF,), 0.5, 3.0, ((0, 32),))
    outer_weight = bell_draw(key_list[14], (FF, D), FF ** -0.5, 0.109375, ((0, 32),))
    outer_bias = bell_draw(key_list[15], (D,), 0.5, 3.0, ((0, 32),))
    final_gain = jnp.clip(1.0 + 0.18 * jax.random.normal(key_list[16], (D,), jnp.float32), 0.099609375, 1.8984375).astype(jnp.bfloat16)
    final_shift = bell_draw(key_list[17], (D,), 0.5, 3.0, ((0, 32),))
    cotangent = bell_draw(key_list[18], (TOKENS, D), 1.0, 6.0, ((0, 32),))
    return {"tokens": tokens, "seq_lengths": seq_lengths, "query_weight": query_weight, "query_bias": query_bias, "key_weight": key_weight, "key_bias": key_bias, "value_weight": value_weight, "value_bias": value_bias, "output_weight": output_weight, "output_bias": output_bias, "norm_gain": norm_gain, "norm_shift": norm_shift, "inner_weight": inner_weight, "inner_bias": inner_bias, "outer_weight": outer_weight, "outer_bias": outer_bias, "final_gain": final_gain, "final_shift": final_shift, "cotangent": cotangent}


@jax.custom_vjp
def low(v):
    return lax.optimization_barrier(v.astype(jnp.bfloat16)).astype(jnp.float32)

@jax.custom_vjp
def low_back(v):
    return v

def low_keep(v):
    return (low(v), None)

def low_pass(kept, grad):
    return (grad,)

def back_keep(v):
    return (v, None)

def back_low(kept, grad):
    return (low(grad),)
low.defvjp(low_keep, low_pass)
low_back.defvjp(back_keep, back_low)
HIGH = lax.Precision.HIGHEST

def geometry(lengths, count):
    lengths = lengths.astype(jnp.int32)
    ends = jnp.cumsum(lengths).astype(jnp.int32)
    starts = (ends - lengths).astype(jnp.int32)
    places = jnp.arange(count, dtype=jnp.int32)
    segment = lax.optimization_barrier(jnp.sum((places[:, None] >= ends[None, :]).astype(jnp.int32), axis=1)).astype(jnp.int32)
    onehot = segment[:, None] == jnp.arange(lengths.shape[0], dtype=jnp.int32)[None, :]
    begin = lax.optimization_barrier(jnp.sum(jnp.where(onehot, starts[None, :], 0), axis=1)).astype(jnp.int32)
    total = lax.optimization_barrier(jnp.sum(jnp.where(onehot, lengths[None, :], 0), axis=1)).astype(jnp.int32)
    angle = 0.5 * math.pi * (places - begin).astype(jnp.float32) / total.astype(jnp.float32)
    return (segment, jnp.cos(angle), jnp.sin(angle))

def layer_norm(hidden, gain, shift):
    center = hidden - lax.optimization_barrier(jnp.mean(hidden, axis=-1, keepdims=True))
    spread = lax.optimization_barrier(jnp.mean(center * center, axis=-1, keepdims=True))
    return center * lax.rsqrt(spread + 1e-05) * gain + shift

def mix_buffer(inputs):
    queries, keys, values, segment, cosine, sine = inputs
    fq = jax.nn.softplus(queries)
    fk = jax.nn.softplus(keys)
    qcos = low_back(low(fq * cosine[:, None, None]))
    qsin = low_back(low(fq * sine[:, None, None]))
    kcos = low_back(low(fk * cosine[:, None, None]))
    ksin = low_back(low(fk * sine[:, None, None]))
    scores = jnp.einsum('ihd,jhd->hij', qcos, kcos, precision=HIGH) + jnp.einsum('ihd,jhd->hij', qsin, ksin, precision=HIGH)
    rows = jnp.arange(queries.shape[0], dtype=jnp.int32)
    allowed = (rows[None, :] <= rows[:, None]) & (segment[:, None] == segment[None, :])
    scores = jnp.where(allowed[None], scores, 0.0)
    numer = jnp.einsum('hij,jhd->ihd', scores, values, precision=HIGH)
    denom = lax.optimization_barrier(jnp.sum(scores, axis=2)).T
    return numer / denom[:, :, None]

def forward(x, query_weight, query_bias, key_weight, key_bias, value_weight, value_bias, output_weight, output_bias, norm_gain, norm_shift, inner_weight, inner_bias, outer_weight, outer_bias, final_gain, final_shift, segment, cosine, sine):

    def project(a, w, b):
        return jnp.dot(a, w, precision=HIGH) + b
    queries = low_back(low(project(x, query_weight, query_bias)))
    keys = low_back(low(project(x, key_weight, key_bias)))
    values = low_back(low(project(x, value_weight, value_bias)))
    shape = (DEVICES, TOK_DEV, HEADS, HD)
    mixed = lax.map(jax.checkpoint(mix_buffer), (queries.reshape(shape), keys.reshape(shape), values.reshape(shape), segment, cosine, sine))
    mixed = low(mixed.reshape(TOKENS, D))
    first = x + low_back(project(mixed, output_weight, output_bias))
    normed = layer_norm(first, norm_gain, norm_shift)
    inner = low_back(project(low(normed), inner_weight, inner_bias))
    activated = low(jax.nn.gelu(inner))
    second = normed + low_back(project(activated, outer_weight, outer_bias))
    return layer_norm(second, final_gain, final_shift)

def reference(tokens, seq_lengths, query_weight, query_bias, key_weight, key_bias, value_weight, value_bias, output_weight, output_bias, norm_gain, norm_shift, inner_weight, inner_bias, outer_weight, outer_bias, final_gain, final_shift, cotangent):
    segment, cosine, sine = jax.vmap(lambda lens: geometry(lens, TOK_DEV))(seq_lengths)
    params = [query_weight, query_bias, key_weight, key_bias, value_weight, value_bias, output_weight, output_bias, norm_gain, norm_shift, inner_weight, inner_bias, outer_weight, outer_bias, final_gain, final_shift]
    params = [p.astype(jnp.float32) for p in params]

    def wrapped(x, *weights):
        return forward(x, *weights, segment, cosine, sine)
    result, pullback = jax.vjp(wrapped, tokens.astype(jnp.float32), *params)
    grads = pullback(cotangent.astype(jnp.float32))
    return (result.astype(jnp.bfloat16), grads[0].astype(jnp.bfloat16), grads[1], grads[2], grads[3], grads[4], grads[5], grads[6], grads[7], grads[8], grads[9], grads[10], grads[11], grads[12], grads[13], grads[14], grads[15], grads[16])
```

```python
import math

import jax
import jax.numpy as jnp
from jax import lax
from jax.experimental import pallas as pl
from jax.experimental.pallas import tpu as pltpu
from jax.sharding import PartitionSpec as P

BF = jnp.bfloat16
F32 = jnp.float32
MESH = pl.DeviceIdType.MESH
AXES = ("dp", "shard")
D = 768
FF = 3072
HD = 64
T = 1024
B = 256
NB = T // B
GROUPS = 32
ROWS = D // GROUPS
MIB = 2**20


def nt(a, b):
    return lax.dot_general(a, b, (((1,), (1,)), ((), ())), preferred_element_type=F32)


def nn(a, b):
    return jnp.dot(a, b, preferred_element_type=F32)


def tn(a, b):
    return lax.dot_general(a, b, (((0,), (0,)), ((), ())), preferred_element_type=F32)


def softplus(x):
    return jnp.maximum(x, 0.0) + jnp.log1p(jnp.exp(-jnp.abs(x)))


CORE = 3
SMALL = "s"
NAMES = "sqkvoiu"
SHAPES = {a: (ROWS, D) for a in "qkvo"}
SHAPES["i"] = (ROWS, FF)
SHAPES["u"] = (FF // GROUPS, D)
SHAPES["s"] = (16, 128)
GATHER_ORDER = {"A": (0, 1, 2, 4), "B": (0, 1, 4, 2), "C": (4, 2, 0, 1)}
SCATTER_ORDER = {"A": (3, 4, 2, 1, 0), "B": (3, 2, 4, 1, 0), "C": (3, 1, 0, 2, 4)}
PARTS = {a: (("A", 0, 384), ("B", 384, 384)) for a in "qkvo"}
PARTS["i"] = (("A", 0, 1024), ("B", 1024, 1024), ("C", 2048, 1024))
PARTS["u"] = (("A", 0, 256), ("B", 256, 256), ("C", 512, 256))
PARTS["s"] = (("A", 0, 128),)
GATHER_CHUNKS = ["sqkv", "o", "i", "u"]
SCATTER_CHUNKS = ["u", "i", "o", "sqkv"]


def job_table(steps):
    table = {}
    for a in NAMES:
        for part in range(len(PARTS[a])):
            for s in range(steps):
                table[a, part, s] = len(table)
    return table


GATHER_JOBS = job_table(6)
SCATTER_JOBS = job_table(5)


class Where:
    def __init__(self, lanes):
        self.dp = lax.axis_index("dp")
        self.shard = lax.axis_index("shard")
        self.lanes = lanes
        group = (self.dp * 2 + self.shard) // lanes
        self.bits = [lax.rem(group // (16 >> e), 2) for e in range(5)]

    def partner(self, e):
        step = (16 >> e) * self.lanes
        if step == 1:
            return (self.dp, 1 - self.shard)
        step = step // 2
        return (self.dp + step - 2 * step * self.bits[e], self.shard)

    def barrier(self):
        bar = pltpu.get_barrier_semaphore()
        for e in range(5):
            pl.semaphore_signal(
                bar, inc=1, device_id=self.partner(e), device_id_type=MESH
            )
        pl.semaphore_wait(bar, 5)


class Gather:
    def __init__(self, where, shards, bufs, send, recv, loc):
        self.where = where
        self.shards = shards
        self.bufs = bufs
        self.send = send
        self.recv = recv
        self.loc = loc

    def view(self, a, full, start, size, flip=None):
        index = []
        for e in range(5):
            bit = self.where.bits[e]
            index.append(slice(None) if e in full else (1 - bit if e == flip else bit))
        return self.bufs[a].at[tuple(index) + (slice(None), pl.ds(start, size))]

    def local(self, a):
        return pltpu.make_async_copy(
            self.shards[a], self.view(a, (), 0, SHAPES[a][1]), self.loc.at[NAMES.index(a)]
        )

    def job(self, a, part, s):
        name, start, size = PARTS[a][part]
        order = GATHER_ORDER[name]
        n = GATHER_JOBS[a, part, s]
        e = order[s] if s < 4 else CORE
        if s < 4:
            dst = self.view(a, order[:s], start, size)
        elif s == 4:
            dst = self.view(a, order[:3], start, size)
        else:
            dst = self.view(a, order[:3], start, size, flip=order[3])
        src = self.shards[a].at[:, pl.ds(start, size)] if s == 0 else dst
        return pltpu.make_async_remote_copy(
            src_ref=src,
            dst_ref=dst,
            send_sem=self.send.at[n],
            recv_sem=self.recv.at[n],
            device_id=self.where.partner(e),
            device_id_type=MESH,
        )

    def step(self, chunk, s):
        for a in chunk:
            if s == 1:
                self.local(a).wait()
            for part in range(len(PARTS[a])):
                if 0 < s <= 4:
                    self.job(a, part, s - 1).wait_recv()
                if s < 4:
                    self.job(a, part, s).start()
                if s >= 3:
                    self.job(a, part, s + 1).start()

    def finish(self, chunk):
        for a in chunk:
            for part in range(len(PARTS[a])):
                self.job(a, part, 4).wait_recv()
                self.job(a, part, 5).wait_recv()

    def drain(self):
        for a in NAMES:
            for part in range(len(PARTS[a])):
                for s in range(6):
                    self.job(a, part, s).wait_send()


def gather_kernel(lanes, *refs):
    n = len(NAMES)
    shards = dict(zip(NAMES, refs[:n]))
    bufs = dict(zip(NAMES, refs[n : 2 * n]))
    gather = Gather(Where(lanes), shards, bufs, *refs[2 * n :])
    for a in NAMES:
        gather.local(a).start()
    gather.where.barrier()
    for t in range(len(GATHER_CHUNKS) + 4):
        for c, chunk in enumerate(GATHER_CHUNKS):
            if 0 <= t - c <= 4:
                gather.step(chunk, t - c)
    for chunk in GATHER_CHUNKS:
        gather.finish(chunk)
    gather.drain()


def all_gather(lanes, arrays):
    anywhere = pl.BlockSpec(memory_space=pl.ANY)
    jobs = len(GATHER_JOBS)
    return pl.pallas_call(
        lambda *refs: gather_kernel(lanes, *refs),
        out_shape=tuple(
            jax.ShapeDtypeStruct((2,) * 5 + SHAPES[a], BF) for a in NAMES
        ),
        in_specs=[anywhere] * len(NAMES),
        out_specs=(anywhere,) * len(NAMES),
        scratch_shapes=[
            pltpu.SemaphoreType.DMA((jobs,)),
            pltpu.SemaphoreType.DMA((jobs,)),
            pltpu.SemaphoreType.DMA((len(NAMES),)),
        ],
        compiler_params=pltpu.CompilerParams(collective_id=3, has_side_effects=True),
        name="gather",
    )(*arrays)


class Scatter:
    def __init__(self, where, grads, landing, send, recv):
        self.where = where
        self.grads = grads
        self.landing = landing
        self.send = send
        self.recv = recv

    def index(self, a, part, s, flip):
        name, start, size = PARTS[a][part]
        order = SCATTER_ORDER[name]
        index = []
        for e in range(5):
            bit = self.where.bits[e]
            if e == order[s]:
                index.append(1 - bit if flip else bit)
            else:
                index.append(bit if e in order[:s] else slice(None))
        return tuple(index), (slice(None), pl.ds(start, size)), order[s]

    def job(self, a, part, s):
        index, block, e = self.index(a, part, s, True)
        n = SCATTER_JOBS[a, part, s]
        return pltpu.make_async_remote_copy(
            src_ref=self.grads[a].at[index + block],
            dst_ref=self.landing[a][s].at[(slice(None),) * (4 - s) + block],
            send_sem=self.send.at[n],
            recv_sem=self.recv.at[n],
            device_id=self.where.partner(e),
            device_id_type=MESH,
        )

    def add(self, a, part, s):
        index, block, _ = self.index(a, part, s, False)
        free = [e for e in range(5) if isinstance(index[e], slice)]
        grads, landing = self.grads[a], self.landing[a][s]

        def one(t, _):
            bits = [lax.rem(t // (1 << (3 - s - k)), 2) for k in range(4 - s)]
            at = list(index)
            for k, e in enumerate(free):
                at[e] = bits[k]
            at = tuple(at) + block
            grads[at] = grads[at] + landing[tuple(bits) + block]
            return 0

        lax.fori_loop(0, 1 << (4 - s), one, 0)

    def step(self, chunk, s):
        for a in chunk:
            for part in range(len(PARTS[a])):
                if s > 0:
                    self.job(a, part, s - 1).wait_recv()
                    self.add(a, part, s - 1)
                if s < 5:
                    self.job(a, part, s).start()

    def drain(self):
        for a in NAMES:
            for part in range(len(PARTS[a])):
                for s in range(5):
                    self.job(a, part, s).wait_send()


def scatter_kernel(lanes, *refs):
    n = len(NAMES)
    given = dict(zip(NAMES, refs[:n]))
    outs = dict(zip(NAMES, refs[n : 2 * n]))
    grads = dict(zip(NAMES, refs[2 * n : 3 * n]))
    rest = refs[3 * n :]
    landing = {a: rest[5 * i : 5 * i + 5] for i, a in enumerate(NAMES)}
    send, recv, loc = rest[5 * n :]

    def load(a):
        return pltpu.make_async_copy(given[a], grads[a], loc.at[NAMES.index(a)])

    for chunk in SCATTER_CHUNKS:
        for a in chunk:
            load(a).start()
    scatter = Scatter(Where(lanes), grads, landing, send, recv)
    scatter.where.barrier()
    for t in range(len(SCATTER_CHUNKS) + 5):
        for c, chunk in enumerate(SCATTER_CHUNKS):
            if t == c:
                for a in chunk:
                    load(a).wait()
            if 0 <= t - c <= 5:
                scatter.step(chunk, t - c)
    for a in NAMES:
        outs[a][...] = grads[a][tuple(scatter.where.bits)].astype(F32)
    scatter.drain()


def reduce_scatter(lanes, grads):
    anywhere = pl.BlockSpec(memory_space=pl.ANY)
    vmem = pl.BlockSpec(memory_space=pltpu.VMEM)
    kind = {a: F32 if a == SMALL else BF for a in NAMES}
    scratch = [pltpu.VMEM((2,) * 5 + SHAPES[a], kind[a]) for a in NAMES]
    for a in NAMES:
        for s in range(5):
            scratch.append(pltpu.VMEM((2,) * (4 - s) + SHAPES[a], kind[a]))
    jobs = len(SCATTER_JOBS)
    scratch += [
        pltpu.SemaphoreType.DMA((jobs,)),
        pltpu.SemaphoreType.DMA((jobs,)),
        pltpu.SemaphoreType.DMA((len(NAMES),)),
    ]
    return pl.pallas_call(
        lambda *refs: scatter_kernel(lanes, *refs),
        out_shape=tuple(jax.ShapeDtypeStruct(SHAPES[a], F32) for a in NAMES),
        in_specs=[anywhere] * len(NAMES),
        out_specs=(vmem,) * len(NAMES),
        scratch_shapes=scratch,
        compiler_params=pltpu.CompilerParams(
            collective_id=4, has_side_effects=True, vmem_limit_bytes=60 * MIB
        ),
        name="scatter",
    )(*grads)


def attention_kernel(c_ref, q_ref, k_ref, v_ref, o_ref, rd_ref, fq, fk0, fk1, v0, v1):
    left = lax.broadcasted_iota(jnp.int32, (T, 128), 1) < 64
    left_block = lax.broadcasted_iota(jnp.int32, (B, 128), 1) < 64

    def pair(hp, _):
        sl = pl.ds(pl.multiple_of(hp * 128, 128), 128)
        fq[...] = softplus(q_ref[:, sl].astype(F32)).astype(BF)
        sk = softplus(k_ref[:, sl].astype(F32))
        fk0[...] = jnp.where(left, sk, 0.0).astype(BF)
        fk1[...] = jnp.where(left, 0.0, sk).astype(BF)
        vv = v_ref[:, sl].astype(F32)
        v0[...] = jnp.where(left, vv, 1.0).astype(BF)
        v1[...] = jnp.where(left, 1.0, vv).astype(BF)
        for i in range(NB):
            r, w = slice(i * B, (i + 1) * B), slice(0, (i + 1) * B)
            sums = []
            for fk, vx in ((fk0, v0), (fk1, v1)):
                weight = nt(fq[r], fk[w]).astype(BF) * c_ref[r, w]
                sums.append(nn(weight, vx[w]))
            numer = jnp.where(left_block, sums[0], sums[1])
            denom = pltpu.roll(jnp.where(left_block, sums[1], sums[0]), 64, 1)
            rd = 1.0 / denom
            o_ref[r, sl] = numer * rd
            rd_ref[r, sl] = rd
        return 0

    lax.fori_loop(0, D // 128, pair, 0)


def attention(c, q, k, v):
    vmem = pl.BlockSpec(memory_space=pltpu.VMEM)
    return pl.pallas_call(
        attention_kernel,
        out_shape=(jax.ShapeDtypeStruct((T, D), F32),) * 2,
        in_specs=[vmem] * 4,
        out_specs=(vmem,) * 2,
        scratch_shapes=[pltpu.VMEM((T, 128), BF)] * 5,
        compiler_params=pltpu.CompilerParams(vmem_limit_bytes=50 * MIB),
        name="attention",
    )(c, q, k, v)


def attention_back_kernel(
    ct_ref, q_ref, k_ref, v_ref, o_ref, rd_ref, gm_ref, gq_ref, gk_ref, gv_ref,
    fq, fk0, fk1, v0, v1, g0, g1, e0, e1, aq,
):
    lane = lax.broadcasted_iota(jnp.int32, (T, 128), 1)
    left = lane < 64
    left_block = lax.broadcasted_iota(jnp.int32, (B, 128), 1) < 64

    def pair(hp, _):
        sl = pl.ds(pl.multiple_of(hp * 128, 128), 128)
        fq[...] = softplus(q_ref[:, sl].astype(F32)).astype(BF)
        sk = softplus(k_ref[:, sl].astype(F32))
        fk0[...] = jnp.where(left, sk, 0.0).astype(BF)
        fk1[...] = jnp.where(left, 0.0, sk).astype(BF)
        vv = v_ref[:, sl].astype(F32)
        v0[...] = jnp.where(left, vv, 1.0).astype(BF)
        v1[...] = jnp.where(left, 1.0, vv).astype(BF)
        gn = (gm_ref[:, sl].astype(F32) * rd_ref[:, sl]).astype(BF).astype(F32)
        through = gn * o_ref[:, sl]
        d0 = -jnp.sum(jnp.where(left, through, 0.0), axis=1, keepdims=True)
        d1 = -jnp.sum(jnp.where(left, 0.0, through), axis=1, keepdims=True)
        h0 = d0.astype(BF).astype(F32)
        h1 = d1.astype(BF).astype(F32)
        g0[...] = jnp.where(left, gn, 0.0).astype(BF)
        g1[...] = jnp.where(left, 0.0, gn).astype(BF)
        t0 = jnp.where(lane == 64, h0, jnp.where(lane == 65, d0 - h0, 0.0))
        t1 = jnp.where(lane == 0, h1, jnp.where(lane == 1, d1 - h1, 0.0))
        e0[...] = jnp.where(left, gn, t0).astype(BF)
        e1[...] = jnp.where(left, t1, gn).astype(BF)
        aq[...] = jnp.zeros_like(aq)
        for j in range(NB):
            r, w = slice(j * B, (j + 1) * B), slice(j * B, T)
            keys, values = [], []
            for fk, vx, g, e in ((fk0, v0, g0, e0), (fk1, v1, g1, e1)):
                weight = nt(fk[r], fq[w]).astype(BF) * ct_ref[r, w]
                change = nt(vx[r], e[w]).astype(BF) * ct_ref[r, w]
                values.append(nn(weight, g[w]))
                keys.append(nn(change, fq[w]))
                aq[w] += tn(change, fk[r])
            gv_ref[r, sl] = (values[0] + values[1]).astype(BF)
            gk = jnp.where(left_block, keys[0], keys[1])
            gk_ref[r, sl] = (gk * jax.nn.sigmoid(k_ref[r, sl].astype(F32))).astype(BF)
        gq_ref[:, sl] = (aq[...] * jax.nn.sigmoid(q_ref[:, sl].astype(F32))).astype(BF)
        return 0

    lax.fori_loop(0, D // 128, pair, 0)


def attention_back(ct, q, k, v, o, rd, gm):
    vmem = pl.BlockSpec(memory_space=pltpu.VMEM)
    return pl.pallas_call(
        attention_back_kernel,
        out_shape=(jax.ShapeDtypeStruct((T, D), BF),) * 3,
        in_specs=[vmem] * 7,
        out_specs=(vmem,) * 3,
        scratch_shapes=[pltpu.VMEM((T, 128), BF)] * 9 + [pltpu.VMEM((T, 128), F32)],
        compiler_params=pltpu.CompilerParams(vmem_limit_bytes=56 * MIB),
        name="attention_back",
    )(ct, q, k, v, o, rd, gm)


def geometry(lengths, count):
    number = lengths.shape[0]
    order = jnp.arange(number, dtype=jnp.int32)
    upto = order[:, None] <= order[None, :]
    ends = jnp.sum(jnp.where(upto, lengths[:, None], 0), axis=0)
    starts = ends - lengths
    places = jnp.arange(count, dtype=jnp.int32)
    segment = jnp.sum((places[:, None] >= ends[None, :]).astype(jnp.int32), axis=1)
    onehot = segment[:, None] == order[None, :]
    begin = jnp.sum(jnp.where(onehot, starts[None, :], 0), axis=1)
    total = jnp.sum(jnp.where(onehot, lengths[None, :], 0), axis=1)
    angle = 0.5 * math.pi * (places - begin).astype(F32) / total.astype(F32)
    return segment, jnp.cos(angle), jnp.sin(angle)


def turn_matrix(segment, cosine, sine, transposed):
    rows = jnp.arange(segment.shape[0], dtype=jnp.int32)
    before = rows[None, :] <= rows[:, None]
    if transposed:
        before = rows[None, :] >= rows[:, None]
    allowed = before & (segment[:, None] == segment[None, :])
    turn = cosine[:, None] * cosine[None, :] + sine[:, None] * sine[None, :]
    return jnp.where(allowed, turn, 0.0).astype(BF)


def layer_norm(hidden, gain, shift):
    center = hidden - jnp.mean(hidden, axis=-1, keepdims=True)
    spread = jnp.mean(center * center, axis=-1, keepdims=True)
    return center * lax.rsqrt(spread + 1e-05) * gain + shift


def column_sums(grad):
    return jnp.sum(grad.astype(F32), axis=0)


def group_gather(x, lanes):
    if lanes > 1:
        x = lax.all_gather(x, "shard", axis=0, tiled=True)
    if lanes > 2:
        size = lanes // 2
        count = lax.axis_size("dp")
        parts = [list(range(i, i + size)) for i in range(0, count, size)]
        x = lax.all_gather(x, "dp", axis=0, tiled=True, axis_index_groups=parts)
    return x


def group_scatter(x, lanes):
    if lanes > 2:
        size = lanes // 2
        count = lax.axis_size("dp")
        parts = [list(range(i, i + size)) for i in range(0, count, size)]
        x = lax.psum_scatter(
            x, "dp", scatter_dimension=0, tiled=True, axis_index_groups=parts
        )
    if lanes > 1:
        x = lax.psum_scatter(x, "shard", scatter_dimension=0, tiled=True)
    return x


def body(
    lanes, tokens, seq_lengths,
    query_weight, query_bias, key_weight, key_bias, value_weight, value_bias,
    output_weight, output_bias, norm_gain, norm_shift, inner_weight, inner_bias,
    outer_weight, outer_bias, final_gain, final_shift, cotangent,
):
    segment, cosine, sine = geometry(seq_lengths[0], T)
    weights = [
        group_gather(w, lanes)
        for w in (
            query_weight, key_weight, value_weight, output_weight, inner_weight, outer_weight,
        )
    ]
    vectors = [
        group_gather(v, lanes).reshape(-1, ROWS)
        for v in (
            query_bias, key_bias, value_bias, output_bias, norm_gain, norm_shift,
            outer_bias, final_gain, final_shift, inner_bias,
        )
    ]
    small = jnp.pad(jnp.concatenate(vectors, axis=0), ((0, 3), (0, 128 - ROWS)))
    gathered = all_gather(lanes, [small] + weights)
    w_query, w_key, w_value, w_output, w_inner, w_outer = (
        g.reshape(-1, g.shape[-1]) for g in gathered[1:]
    )
    small = gathered[0].reshape(GROUPS, 16, 128)[:, :, :ROWS].astype(F32)
    b_query, b_key, b_value, b_output, g_one, s_one, b_outer, g_two, s_two = (
        small[:, i].reshape(D) for i in range(9)
    )
    b_inner = small[:, 9:13].reshape(FF)
    query = (nn(tokens, w_query) + b_query).astype(BF)
    key = (nn(tokens, w_key) + b_key).astype(BF)
    value = (nn(tokens, w_value) + b_value).astype(BF)
    mixed, inverse = attention(
        turn_matrix(segment, cosine, sine, False), query, key, value
    )
    mixed_low = mixed.astype(BF)
    first = tokens.astype(F32) + nn(mixed_low, w_output) + b_output
    normed, norm_back = jax.vjp(layer_norm, first, g_one, s_one)
    normed_low = normed.astype(BF)
    inner = nn(normed_low, w_inner) + b_inner
    activated, gelu_back = jax.vjp(jax.nn.gelu, inner)
    activated_low = activated.astype(BF)
    second = normed + nn(activated_low, w_outer) + b_outer
    result, final_back = jax.vjp(layer_norm, second, g_two, s_two)
    g_second, final_gain_grad, final_shift_grad = final_back(cotangent.astype(F32))
    g_branch = g_second.astype(BF)
    outer_weight_grad = tn(activated_low, g_branch)
    g_inner = gelu_back(nt(g_branch, w_outer))[0].astype(BF)
    inner_weight_grad = tn(normed_low, g_inner)
    g_normed = g_second + nt(g_inner, w_inner)
    g_first, norm_gain_grad, norm_shift_grad = norm_back(g_normed)
    g_attended = g_first.astype(BF)
    output_weight_grad = tn(mixed_low, g_attended)
    g_mixed = nt(g_attended, w_output)
    g_query, g_key, g_value = attention_back(
        turn_matrix(segment, cosine, sine, True), query, key, value, mixed, inverse, g_mixed
    )
    tokens_grad = g_first + nt(g_query, w_query) + nt(g_key, w_key) + nt(g_value, w_value)
    vector_grads = (
        column_sums(g_query), column_sums(g_key), column_sums(g_value),
        column_sums(g_attended), norm_gain_grad, norm_shift_grad,
        column_sums(g_branch), final_gain_grad, final_shift_grad,
        column_sums(g_inner),
    )
    packed = jnp.concatenate([v.reshape(GROUPS, -1, ROWS) for v in vector_grads], axis=1)
    packed = jnp.pad(packed, ((0, 0), (0, 3), (0, 128 - ROWS)))
    grads = [
        tn(tokens, g_query), tn(tokens, g_key), tn(tokens, g_value),
        output_weight_grad, inner_weight_grad, outer_weight_grad,
    ]
    grads = [packed] + [g.astype(BF) for g in grads]
    shares = reduce_scatter(
        lanes, [g.reshape((2,) * 5 + SHAPES[a]) for a, g in zip(NAMES, grads)]
    )
    vec = [group_scatter(shares[0][i, :ROWS], lanes) for i in range(9)]
    inner_bias_grad = group_scatter(shares[0][9:13, :ROWS].reshape(-1), lanes)
    mat = [group_scatter(s, lanes) for s in shares[1:]]
    return (
        result.astype(BF), tokens_grad.astype(BF),
        mat[0], vec[0], mat[1], vec[1], mat[2], vec[2], mat[3], vec[3],
        vec[4], vec[5], mat[4], inner_bias_grad, mat[5], vec[6], vec[7], vec[8],
    )


def solution(mesh):
    lanes = mesh.shape["dp"] * mesh.shape["shard"] // GROUPS
    rows, flat = P(AXES, None), P(AXES)
    return jax.shard_map(
        lambda *args: body(lanes, *args),
        mesh=mesh,
        in_specs=(rows, rows) + (rows, flat) * 4 + (flat, flat) + (rows, flat) * 2 + (flat, flat, rows),
        out_specs=(rows, rows) + (rows, flat) * 4 + (flat, flat) + (rows, flat) * 2 + (flat, flat),
        check_vma=False,
    )
```

```python
import math

import jax
import jax.numpy as jnp
from jax import lax
from jax.experimental import pallas as pl
from jax.experimental.pallas import tpu as pltpu
from jax.sharding import PartitionSpec as P

BF = jnp.bfloat16
F32 = jnp.float32
MESH = pl.DeviceIdType.MESH
AXES = ("dp", "shard")
D = 768
FF = 3072
HD = 64
T = 1024
B = 256
NB = T // B
GROUPS = 32
ROWS = D // GROUPS
MIB = 2**20


def nt(a, b):
    return lax.dot_general(a, b, (((1,), (1,)), ((), ())), preferred_element_type=F32)


def nn(a, b):
    return jnp.dot(a, b, preferred_element_type=F32)


def tn(a, b):
    return lax.dot_general(a, b, (((0,), (0,)), ((), ())), preferred_element_type=F32)


def softplus(x):
    return jnp.maximum(x, 0.0) + jnp.log1p(jnp.exp(-jnp.abs(x)))


CORE = 3
SMALL = "s"
NAMES = "sqkvoiu"
SHAPES = {a: (ROWS, D) for a in "qkvo"}
SHAPES["i"] = (ROWS, FF)
SHAPES["u"] = (FF // GROUPS, D)
SHAPES["s"] = (16, 128)
LINE = ((0,), (1,), (0, 1))
GATHER_ORDER = {
    "A": (LINE, ((2,),), ((4,),)),
    "B": (LINE, ((4,),), ((2,),)),
    "C": (((4,),), ((2,),), ((0,),), ((1,),)),
}
GATHER_PARTS = {a: (("A", 0, 256), ("B", 256, 256), ("C", 512, 256)) for a in "qkvo"}
GATHER_PARTS["i"] = (("A", 0, 1280), ("B", 1280, 1280), ("C", 2560, 512))
GATHER_PARTS["u"] = (("A", 0, 384), ("B", 384, 384))
GATHER_PARTS["s"] = (("A", 0, 128),)
GATHER_JOBS = {}
for a in NAMES:
    for part, (name, _, _) in enumerate(GATHER_PARTS[a]):
        for s, moves in enumerate(GATHER_ORDER[name] + (((CORE,), (CORE,)),)):
            for move in range(len(moves)):
                GATHER_JOBS[a, part, s, move] = len(GATHER_JOBS)


class Where:
    def __init__(self, lanes):
        self.dp = lax.axis_index("dp")
        self.shard = lax.axis_index("shard")
        self.lanes = lanes
        group = (self.dp * 2 + self.shard) // lanes
        self.bits = [lax.rem(group // (16 >> e), 2) for e in range(5)]

    def partner(self, *flips):
        dp, shard = self.dp, self.shard
        for e in flips:
            step = (16 >> e) * self.lanes
            if step == 1:
                shard = 1 - shard
            else:
                step = step // 2
                dp = dp + step - 2 * step * self.bits[e]
        return (dp, shard)

    def barrier(self, moves=((0,), (1,), (0, 1), (2,), (3,), (4,))):
        bar = pltpu.get_barrier_semaphore()
        for move in moves:
            pl.semaphore_signal(
                bar, inc=1, device_id=self.partner(*move), device_id_type=MESH
            )
        pl.semaphore_wait(bar, len(moves))


class Gather:
    def __init__(self, where, shards, bufs, send, recv, loc):
        self.where = where
        self.shards = shards
        self.bufs = bufs
        self.send = send
        self.recv = recv
        self.loc = loc
        self.placed = set()

    def view(self, a, full, start, size, flip=()):
        index = []
        for e in range(5):
            bit = self.where.bits[e]
            index.append(slice(None) if e in full else (1 - bit if e in flip else bit))
        return self.bufs[a].at[tuple(index) + (slice(None), pl.ds(start, size))]

    def local(self, a):
        return pltpu.make_async_copy(
            self.shards[a], self.view(a, (), 0, SHAPES[a][1]), self.loc.at[NAMES.index(a)]
        )

    def job(self, a, part, s, move):
        name, start, size = GATHER_PARTS[a][part]
        order = GATHER_ORDER[name]
        done = [e for stage in order[: min(s, len(order) - 1)] for m in stage for e in m]
        if s < len(order):
            flips = order[s][move]
            dst = self.view(a, done, start, size)
        else:
            flips = (CORE,)
            dst = self.view(a, done, start, size, flip=order[-1][0] if move else ())
        src = self.shards[a].at[:, pl.ds(start, size)] if s == 0 else dst
        n = GATHER_JOBS[a, part, s, move]
        return pltpu.make_async_remote_copy(
            src_ref=src,
            dst_ref=dst,
            send_sem=self.send.at[n],
            recv_sem=self.recv.at[n],
            device_id=self.where.partner(*flips),
            device_id_type=MESH,
        )

    def step(self, a, s):
        if s == 1 and a not in self.placed:
            self.placed.add(a)
            self.local(a).wait()
        for part, (name, _, _) in enumerate(GATHER_PARTS[a]):
            order = GATHER_ORDER[name]
            last = len(order)
            if 0 < s <= last:
                for move in range(len(order[s - 1])):
                    self.job(a, part, s - 1, move).wait_recv()
            if s < last:
                for move in range(len(order[s])):
                    self.job(a, part, s, move).start()
            if s == last - 1:
                self.job(a, part, last, 0).start()
            if s == last:
                self.job(a, part, last, 1).start()
            if s == last + 1:
                self.job(a, part, last, 0).wait_recv()
                self.job(a, part, last, 1).wait_recv()

    def drain(self):
        for key in GATHER_JOBS:
            self.job(*key).wait_send()


SCATTER_ORDER = {
    "A": (((CORE,),), ((4,),), ((2,),), LINE),
    "B": (((CORE,),), ((2,),), ((4,),), LINE),
}
INNER_PARTS = {f"i{m}{h}": (h, ROWS, 384) for m in range(4) for h in "AB"}
LATE_PARTS = {f"u{c}{h}": (h, 4 * ROWS, 128) for c in range(3) for h in "AB"}
LATE_PARTS.update({f"o{h}": (h, ROWS, 384) for h in "AB"})
HEAD_PARTS = {f"h{c}{h}": (h, 3 * ROWS, 128) for c in range(3) for h in "AB"}
TAIL_PARTS = {**LATE_PARTS, **HEAD_PARTS}


def scatter_jobs(parts):
    jobs = {}
    for name, (kind, _, _) in parts.items():
        for s, moves in enumerate(SCATTER_ORDER[kind]):
            for move in range(len(moves)):
                jobs[name, s, move] = len(jobs)
    return jobs


def scatter_scratch(parts):
    scratch = []
    for _, rows, size in parts.values():
        scratch += [
            pltpu.VMEM(dims + (rows, size), BF)
            for dims in ((2,) * 5, (2,) * 4, (2,) * 3, (2,) * 2, (3,))
        ]
    jobs = len(scatter_jobs(parts))
    return scratch + [pltpu.SemaphoreType.DMA((jobs,)), pltpu.SemaphoreType.DMA((jobs,))]


def scatter_count(parts):
    return 5 * len(parts) + 2


class Scatter:
    def __init__(self, where, parts, refs):
        self.where = where
        self.parts = parts
        self.grads = {name: refs[5 * i] for i, name in enumerate(parts)}
        self.landing = {name: refs[5 * i + 1 : 5 * i + 5] for i, name in enumerate(parts)}
        self.send, self.recv = refs[5 * len(parts) :]
        self.jobs = scatter_jobs(parts)

    def index(self, name, s, flips):
        order = SCATTER_ORDER[self.parts[name][0]]
        moved = [e for stage in order[: s + 1] for m in stage for e in m]
        index = []
        for e in range(5):
            bit = self.where.bits[e]
            index.append((1 - bit if e in flips else bit) if e in moved else slice(None))
        return tuple(index)

    def job(self, name, s, move):
        flips = SCATTER_ORDER[self.parts[name][0]][s][move]
        n = self.jobs[name, s, move]
        landing = self.landing[name][s]
        return pltpu.make_async_remote_copy(
            src_ref=self.grads[name].at[self.index(name, s, flips)],
            dst_ref=landing.at[move] if s == 3 else landing,
            send_sem=self.send.at[n],
            recv_sem=self.recv.at[n],
            device_id=self.where.partner(*flips),
            device_id_type=MESH,
        )

    def add(self, name, s):
        index = self.index(name, s, ())
        grads, landing = self.grads[name], self.landing[name][s]
        if s == 3:
            total = grads[index].astype(F32)
            for move in range(3):
                total = total + landing[move].astype(F32)
            grads[index] = total.astype(BF)
            return
        free = [e for e in range(5) if isinstance(index[e], slice)]

        def one(t, _):
            bits = [lax.rem(t // (1 << (3 - s - k)), 2) for k in range(4 - s)]
            at = list(index)
            for k, e in enumerate(free):
                at[e] = bits[k]
            grads[tuple(at)] = grads[tuple(at)] + landing[tuple(bits)]
            return 0

        lax.fori_loop(0, 1 << (4 - s), one, 0)

    def step(self, name, s):
        for half in "AB":
            part = name + half
            moves = SCATTER_ORDER[half]
            if s > 0:
                for move in range(len(moves[s - 1])):
                    self.job(part, s - 1, move).wait_recv()
                self.add(part, s - 1)
            if s < 4:
                for move in range(len(moves[s])):
                    self.job(part, s, move).start()

    def steps(self, *names):
        for name in names:
            self.step(name[:-1], int(name[-1]))

    def own(self, part):
        return self.grads[part][tuple(self.where.bits)].astype(F32)

    def drain(self):
        for key in self.jobs:
            self.job(*key).wait_send()


def spread(dst, value, rows, at):
    dims = len(dst.shape) - 2
    for g in range(1 << dims):
        bits = tuple((g >> (dims - 1 - e)) & 1 for e in range(dims))
        dst[bits + (slice(at, at + rows),)] = value[g * rows : (g + 1) * rows].astype(BF)


BEFORE = (
    "sqk0", "sqk1", "v0", "sqk2", "v1", "oi0", "sqk3", "v2", "sqk4", "v3", "oi1",
    "qk5", "v4", "u0", "v5",
)
BETWEEN = {1: ("oi3", "u2"), 2: ("oi4",), 3: ("oi5",), 5: ("u3",)}


def rows_of(t, size):
    return pl.ds(pl.multiple_of(t * size, size), size)


def assemble(w, staged):
    for g in range(GROUPS):
        bits = tuple((g >> (4 - e)) & 1 for e in range(5))
        w[g * ROWS : (g + 1) * ROWS, :] = staged[bits]


def fill_turn(c_ref, col_ref, row_ref, transposed):
    for i in range(NB):
        for j in range(NB):
            if (j < i) if transposed else (j > i):
                continue
            r, w = slice(i * B, (i + 1) * B), slice(j * B, (j + 1) * B)
            turn = col_ref[r, 0:1] * row_ref[0:1, w] + col_ref[r, 1:2] * row_ref[1:2, w]
            allowed = col_ref[r, 2:3] == row_ref[2:3, w]
            if i == j:
                mine = lax.broadcasted_iota(jnp.int32, (B, B), 0)
                other = lax.broadcasted_iota(jnp.int32, (B, B), 1)
                allowed &= (other >= mine) if transposed else (other <= mine)
            c_ref[r, w] = jnp.where(allowed, turn, 0.0).astype(BF)


def normalize(h):
    center = h - jnp.mean(h, axis=1, keepdims=True)
    rstd = lax.rsqrt(jnp.mean(center * center, axis=1, keepdims=True) + 1e-05)
    return center * rstd, rstd


def forward_kernel(lanes, *refs):
    n = len(NAMES)
    shards = dict(zip(NAMES, refs[:n]))
    x, col, row, cot = refs[n : n + 4]
    refs = refs[n + 4 :]
    bufs = dict(zip("qkvoiu", refs[:6]))
    (
        q, k, v, o, rd, mixed, hat, rstd, low, inner, result, g_second, vec, sums,
        small, staged, w, c, fq, fk0, fk1, v0, v1, acc, act, b_inner,
        send, recv, loc, load,
    ) = refs[6:]
    bufs["s"] = small
    gather = Gather(Where(lanes), shards, bufs, send, recv, loc)
    for a in NAMES:
        gather.local(a).start()
    gather.where.barrier()

    def steps(*names):
        for name in names:
            for a in name[:-1]:
                gather.step(a, int(name[-1]))

    def stage(i):
        if i < 4:
            src = bufs["qkvo"[i]]
        else:
            src = bufs["i"].at[(slice(None),) * 6 + (pl.ds((i - 4) * D, D),)]
        return pltpu.make_async_copy(src, staged.at[i % 2], load.at[i % 2])

    def stage_outer(m):
        return [
            pltpu.make_async_copy(
                bufs["u"].at[m // 2, m % 2, p // 4, p // 2 % 2, p % 2],
                w.at[m % 2, pl.ds(p * (FF // GROUPS), FF // GROUPS)],
                load.at[2 + 8 * (m % 2) + p],
            )
            for p in range(8)
        ]

    fill_turn(c, col, row, False)
    steps(*BEFORE)
    stage(0).start()
    vec[...] = jnp.zeros_like(vec)
    b_inner[...] = jnp.zeros_like(b_inner)
    lane = lax.broadcasted_iota(jnp.int32, (16, 256), 1)
    for g in range(GROUPS):
        bits = tuple((g >> (4 - e)) & 1 for e in range(5))
        mine = small[bits].astype(F32)
        mine = jnp.concatenate([mine, jnp.zeros_like(mine)], axis=1)
        for dst, rows, width in ((vec, slice(0, 16), ROWS), (b_inner, slice(8, 16), 4 * ROWS)):
            at = g * width
            piece = jnp.where(lane < width, mine, 0.0)
            if at % 128:
                piece = pltpu.roll(piece, at % 128, 1)
            at = at // 128 * 128
            dst[:, at : at + 256] += piece[rows]
    for i, (name, out) in enumerate(zip("qkv", (q, k, v))):
        stage(i).wait()
        if i < 2:
            stage(i + 1).start()
        assemble(w.at[0], staged.at[i % 2])
        for at in range(0, D, 256):
            out[:, at : at + 256] = (
                nn(x[...], w[0, :, at : at + 256]) + vec[i : i + 1, at : at + 256]
            ).astype(BF)
        if i == 0:
            steps("oi2", "u1")

    def between(hp):
        for at, names in BETWEEN.items():
            pl.when(hp == at)(lambda names=names: steps(*names))

    attend(c, q, k, v, o, rd, fq, fk0, fk1, v0, v1, between)
    stage(3).start()
    stage(3).wait()
    stage(4).start()
    assemble(w.at[0], staged.at[1])

    def attended(t, _):
        r = rows_of(t, B)
        low_mixed = o[r, :].astype(BF)
        mixed[r, :] = low_mixed
        first = x[r, :].astype(F32) + nn(low_mixed, w[0]) + vec[3:4, :D]
        xhat, spread = normalize(first)
        hat[r, :] = xhat.astype(BF)
        rstd[r, :] = jnp.broadcast_to(spread, (B, 128))
        normed = xhat * vec[4:5, :D] + vec[5:6, :D]
        low[r, :] = normed.astype(BF)
        acc[r, :] = normed + vec[6:7, :D]
        return 0

    lax.fori_loop(0, NB, attended, 0)
    for j in range(4):
        stage(4 + j).wait()
        if j < 3:
            stage(5 + j).start()
        assemble(w.at[0], staged.at[j % 2])
        for at in range(0, D, 256):
            hidden = nn(low[...], w[0, :, at : at + 256]) + b_inner[1:2, j * D + at : j * D + at + 256]
            inner[:, j * D + at : j * D + at + 256] = hidden.astype(BF)
            act[:, j * D + at : j * D + at + 256] = jax.nn.gelu(hidden).astype(BF)
    steps("u4", "u5")
    for m in range(4):
        for copy in stage_outer(m):
            copy.start()
        for copy in stage_outer(m):
            copy.wait()
        for at in range(0, D, 256):
            acc[:, at : at + 256] += nn(act[:, m * D : (m + 1) * D], w[m % 2, :, at : at + 256])
    sums[...] = jnp.zeros_like(sums)

    def final(t, _):
        r = rows_of(t, 128)
        xhat, spread = normalize(acc[r, :])
        gain = vec[7:8, :D]
        result[r, :] = (xhat * gain + vec[8:9, :D]).astype(BF)
        back = cot[r, :].astype(F32)
        scaled = back * gain
        g = spread * (
            scaled
            - jnp.mean(scaled, axis=1, keepdims=True)
            - xhat * jnp.mean(scaled * xhat, axis=1, keepdims=True)
        )
        g_second[r, :] = g
        sums[0:1, :] += jnp.sum(g.astype(BF).astype(F32), axis=0, keepdims=True)
        sums[1:2, :] += jnp.sum(back * xhat, axis=0, keepdims=True)
        sums[2:3, :] += jnp.sum(back, axis=0, keepdims=True)
        return 0

    lax.fori_loop(0, T // 128, final, 0)
    gather.drain()


def forward(lanes, arrays, x, col, row, cot):
    anywhere = pl.BlockSpec(memory_space=pl.ANY)
    vmem = pl.BlockSpec(memory_space=pltpu.VMEM)
    jobs = len(GATHER_JOBS)
    shape = jax.ShapeDtypeStruct
    rows = shape((T, D), BF)
    wide = shape((T, D), F32)
    outs = [shape((2,) * 5 + SHAPES[a], BF) for a in "qkvoiu"]
    kept = [
        rows, rows, rows, wide, wide, rows, rows, shape((T, 128), F32), rows,
        shape((T, FF), BF), rows, wide, shape((16, D + 128), F32), shape((8, D), F32),
    ]
    return pl.pallas_call(
        lambda *refs: forward_kernel(lanes, *refs),
        out_shape=tuple(outs + kept),
        in_specs=[anywhere] * len(NAMES) + [vmem] * 4,
        out_specs=(anywhere,) * 6 + (vmem,) * len(kept),
        scratch_shapes=[
            pltpu.VMEM((2,) * 5 + SHAPES["s"], BF),
            pltpu.VMEM((2,) + (2,) * 5 + (ROWS, D), BF),
            pltpu.VMEM((2, D, D), BF),
            pltpu.VMEM((T, T), BF),
            *[pltpu.VMEM((T, 128), BF)] * 5,
            pltpu.VMEM((T, D), F32),
            pltpu.VMEM((T, FF), BF),
            pltpu.VMEM((8, FF + 128), F32),
            pltpu.SemaphoreType.DMA((jobs,)),
            pltpu.SemaphoreType.DMA((jobs,)),
            pltpu.SemaphoreType.DMA((len(NAMES),)),
            pltpu.SemaphoreType.DMA((18,)),
        ],
        compiler_params=pltpu.CompilerParams(
            collective_id=3, has_side_effects=True, vmem_limit_bytes=61 * MIB
        ),
        name="forward",
    )(*arrays, x, col, row, cot)


def attend(c_ref, q_ref, k_ref, v_ref, o_ref, rd_ref, fq, fk0, fk1, v0, v1, between):
    left = lax.broadcasted_iota(jnp.int32, (T, 128), 1) < 64
    left_block = lax.broadcasted_iota(jnp.int32, (B, 128), 1) < 64

    def pair(hp, _):
        sl = pl.ds(pl.multiple_of(hp * 128, 128), 128)
        fq[...] = softplus(q_ref[:, sl].astype(F32)).astype(BF)
        sk = softplus(k_ref[:, sl].astype(F32))
        fk0[...] = jnp.where(left, sk, 0.0).astype(BF)
        fk1[...] = jnp.where(left, 0.0, sk).astype(BF)
        vv = v_ref[:, sl].astype(F32)
        v0[...] = jnp.where(left, vv, 1.0).astype(BF)
        v1[...] = jnp.where(left, 1.0, vv).astype(BF)
        for i in range(NB):
            r, w = slice(i * B, (i + 1) * B), slice(0, (i + 1) * B)
            sums = []
            for fk, vx in ((fk0, v0), (fk1, v1)):
                weight = nt(fq[r], fk[w]).astype(BF) * c_ref[r, w]
                sums.append(nn(weight, vx[w]))
            numer = jnp.where(left_block, sums[0], sums[1])
            denom = pltpu.roll(jnp.where(left_block, sums[1], sums[0]), 64, 1)
            rd = 1.0 / denom
            o_ref[r, sl] = numer * rd
            rd_ref[r, sl] = rd
        between(hp)
        return 0

    lax.fori_loop(0, D // 128, pair, 0)


def inner_back_kernel(lanes, *refs):
    (
        g_second, inner, w_outer, low, w_inner, hat, rstd, vec, mixed, w_output, sums_in,
    ) = refs[:11]
    late = dict(zip(LATE_PARTS, refs[11:19]))
    g_low, g_mixed, sums, shares = refs[19:23]
    gn, hid, act, wu, wi, lo, gb, acc_sem = refs[23:31]
    scatter = Scatter(Where(lanes), INNER_PARTS, refs[31:])

    def load(i):
        src, dst = ((g_second, gn), (inner, hid), (w_outer, wu), (low, lo), (w_inner, wi))[i]
        return pltpu.make_async_copy(src, dst, acc_sem.at[i])

    for i in range(5):
        load(i).start()
    scatter.where.barrier()
    sums[...] = sums_in[...]
    load(0).wait()
    gb[...] = gn[...].astype(BF)
    load(1).wait()
    load(2).wait()
    c0 = math.sqrt(2.0 / math.pi)
    for m in range(4):
        for at in range(0, D, 256):
            cols = slice(m * D + at, m * D + at + 256)
            back = nt(gb[...], wu[cols, :])
            h = hid[:, cols].astype(F32)
            square = h * h
            t = jnp.tanh(c0 * h * (1.0 + 0.044715 * square))
            half = 0.5 + 0.5 * t
            act[:, cols] = (h * half).astype(BF)
            slope = half + 0.5 * h * (1.0 - t * t) * (c0 * (1.0 + 3 * 0.044715 * square))
            g = (back * slope).astype(BF)
            hid[:, cols] = g
            sums[9 + m : 10 + m, at : at + 256] = jnp.sum(
                g.astype(F32), axis=0, keepdims=True
            )
        if m == 0:
            load(3).wait()
            load(4).wait()
        for h, half in enumerate("AB"):
            cols = slice(m * D + h * 384, m * D + h * 384 + 384)
            spread(scatter.grads[f"i{m}{half}"], tn(lo[...], hid[:, cols]), ROWS, 0)
        scatter.steps(*INNER_STEPS[2 * m])
        for at in range(0, D, 256):
            gn[:, at : at + 256] += nt(
                hid[:, m * D : (m + 1) * D], wi[at : at + 256, m * D : (m + 1) * D]
            )
        scatter.steps(*INNER_STEPS[2 * m + 1])

    def first_back(t, _):
        r = rows_of(t, 128)
        g = gn[r, :]
        xhat = hat[r, :].astype(F32)
        sums[4:5, :] += jnp.sum(g * xhat, axis=0, keepdims=True)
        sums[5:6, :] += jnp.sum(g, axis=0, keepdims=True)
        scaled = g * vec[4:5, :D]
        g_first = rstd[r, 0:1] * (
            scaled
            - jnp.mean(scaled, axis=1, keepdims=True)
            - xhat * jnp.mean(scaled * xhat, axis=1, keepdims=True)
        )
        g_attended = g_first.astype(BF)
        g_low[r, :] = g_attended
        sums[3:4, :] += jnp.sum(g_attended.astype(F32), axis=0, keepdims=True)
        return 0

    lax.fori_loop(0, T // 128, first_back, 0)
    scatter.steps(*INNER_STEPS[8])
    for at in range(0, D, 256):
        g_mixed[:, at : at + 256] = nt(g_low[...], w_output[at : at + 256, :]).astype(BF)
    for h, half in enumerate("AB"):
        spread(late["o" + half], tn(mixed[...], g_low[:, h * 384 : h * 384 + 384]), ROWS, 0)
    scatter.steps(*INNER_STEPS[9])
    for m in range(4):
        for c in range(3):
            value = tn(act[:, m * D : (m + 1) * D], gb[:, c * 256 : c * 256 + 256])
            for h, half in enumerate("AB"):
                spread(
                    late[f"u{c}{half}"].at[m // 2, m % 2],
                    value[:, h * 128 : h * 128 + 128],
                    4 * ROWS,
                    0,
                )
        if 10 + m < len(INNER_STEPS):
            scatter.steps(*INNER_STEPS[10 + m])
    for m in range(4):
        shares[:, m * D : m * D + 384] = scatter.own(f"i{m}A")
        shares[:, m * D + 384 : (m + 1) * D] = scatter.own(f"i{m}B")
    scatter.drain()


INNER_STEPS = (
    ("i00",), ("i01",),
    ("i02", "i10"), ("i03", "i11"),
    ("i04", "i12", "i20"), ("i13", "i21"),
    ("i14", "i22", "i30"), ("i23", "i31"),
    ("i24", "i32"), ("i33",), (), ("i34",),
)


def inner_back(lanes, g_second, inner, w_outer, low, w_inner, hat, rstd, vec, mixed, w_output, sums):
    anywhere = pl.BlockSpec(memory_space=pl.ANY)
    vmem = pl.BlockSpec(memory_space=pltpu.VMEM)
    shape = jax.ShapeDtypeStruct
    late = [shape((2,) * 5 + p[1:], BF) for p in LATE_PARTS.values()]
    return pl.pallas_call(
        lambda *refs: inner_back_kernel(lanes, *refs),
        out_shape=tuple(
            late
            + [shape((T, D), BF), shape((T, D), BF), shape((16, D), F32), shape((ROWS, FF), F32)]
        ),
        in_specs=[anywhere] * 5 + [vmem] * 6,
        out_specs=(vmem,) * (len(late) + 4),
        scratch_shapes=[
            pltpu.VMEM((T, D), F32),
            pltpu.VMEM((T, FF), BF),
            pltpu.VMEM((T, FF), BF),
            pltpu.VMEM((FF, D), BF),
            pltpu.VMEM((D, FF), BF),
            pltpu.VMEM((T, D), BF),
            pltpu.VMEM((T, D), BF),
            pltpu.SemaphoreType.DMA((5,)),
            *scatter_scratch(INNER_PARTS),
        ],
        compiler_params=pltpu.CompilerParams(
            collective_id=4, has_side_effects=True, vmem_limit_bytes=61 * MIB
        ),
        name="inner_back",
    )(g_second, inner, w_outer, low, w_inner, hat, rstd, vec, mixed, w_output, sums)


def heads_back_kernel(lanes, *refs):
    late = dict(zip(LATE_PARTS, refs[:8]))
    q, k, v, o, rd, gm, x, g_low, wq, wk, wv, col, row, sums_in = refs[8:22]
    tokens_grad, share_q, share_k, share_v, share_o, share_u, sums = refs[22:29]
    (
        ct, gq, gk, gv, fq, fk0, fk1, v0, v1, g0, g1, e0, e1, aq,
        landing, vec_send, vec_recv, load_sem,
    ) = refs[29:47]
    scatter = Scatter(Where(lanes), TAIL_PARTS, refs[47:])
    where = scatter.where

    def load(name):
        return pltpu.make_async_copy(
            late[name], scatter.grads[name], load_sem.at[list(late).index(name)]
        )

    for name in late:
        load(name).start()
    where.barrier()
    for name in late:
        load(name).wait()
    scatter.steps(*TAIL_STEPS[0])
    fill_turn(ct, col, row, True)
    lane = lax.broadcasted_iota(jnp.int32, (T, 128), 1)
    left = lane < 64
    left_block = lax.broadcasted_iota(jnp.int32, (B, 128), 1) < 64

    def pair(hp, _):
        sl = pl.ds(pl.multiple_of(hp * 128, 128), 128)
        fq[...] = softplus(q[:, sl].astype(F32)).astype(BF)
        sk = softplus(k[:, sl].astype(F32))
        fk0[...] = jnp.where(left, sk, 0.0).astype(BF)
        fk1[...] = jnp.where(left, 0.0, sk).astype(BF)
        vv = v[:, sl].astype(F32)
        v0[...] = jnp.where(left, vv, 1.0).astype(BF)
        v1[...] = jnp.where(left, 1.0, vv).astype(BF)
        gn = (gm[:, sl].astype(F32) * rd[:, sl]).astype(BF).astype(F32)
        through = gn * o[:, sl]
        d0 = -jnp.sum(jnp.where(left, through, 0.0), axis=1, keepdims=True)
        d1 = -jnp.sum(jnp.where(left, 0.0, through), axis=1, keepdims=True)
        h0 = d0.astype(BF).astype(F32)
        h1 = d1.astype(BF).astype(F32)
        g0[...] = jnp.where(left, gn, 0.0).astype(BF)
        g1[...] = jnp.where(left, 0.0, gn).astype(BF)
        t0 = jnp.where(lane == 64, h0, jnp.where(lane == 65, d0 - h0, 0.0))
        t1 = jnp.where(lane == 0, h1, jnp.where(lane == 1, d1 - h1, 0.0))
        e0[...] = jnp.where(left, gn, t0).astype(BF)
        e1[...] = jnp.where(left, t1, gn).astype(BF)
        aq[...] = jnp.zeros_like(aq)
        for j in range(NB):
            r, w = slice(j * B, (j + 1) * B), slice(j * B, T)
            keys, values = [], []
            for fk, vx, g, e in ((fk0, v0, g0, e0), (fk1, v1, g1, e1)):
                weight = nt(fk[r], fq[w]).astype(BF) * ct[r, w]
                change = nt(vx[r], e[w]).astype(BF) * ct[r, w]
                values.append(nn(weight, g[w]))
                keys.append(nn(change, fq[w]))
                aq[w] += tn(change, fk[r])
            gv[r, sl] = (values[0] + values[1]).astype(BF)
            back = jnp.where(left_block, keys[0], keys[1])
            gk[r, sl] = (back * jax.nn.sigmoid(k[r, sl].astype(F32))).astype(BF)
            for (at, block), names in TAIL_BETWEEN.items():
                if block == j:
                    pl.when(hp == at)(lambda names=names: scatter.steps(*names))
        gq[:, sl] = (aq[...] * jax.nn.sigmoid(q[:, sl].astype(F32))).astype(BF)
        return 0

    sums[...] = sums_in[...]
    for c in range(3):
        lax.fori_loop(2 * c, 2 * c + 2, pair, 0)
        cols = slice(c * 256, c * 256 + 256)
        for i, g in enumerate((gq, gk, gv)):
            value = tn(x[...], g[:, cols])
            for h, half in enumerate("AB"):
                spread(
                    scatter.grads[f"h{c}{half}"],
                    value[:, h * 128 : h * 128 + 128],
                    ROWS,
                    i * ROWS,
                )
        scatter.steps(f"h{c}0")
        for i, g in enumerate((gq, gk, gv)):
            sums[i : i + 1, cols] = jnp.sum(g[:, cols].astype(F32), axis=0, keepdims=True)

    stages = SCATTER_ORDER["A"]

    def vector(s, move):
        n = s + move
        return pltpu.make_async_remote_copy(
            src_ref=sums,
            dst_ref=landing.at[n],
            send_sem=vec_send.at[n],
            recv_sem=vec_recv.at[n],
            device_id=where.partner(*stages[s][move]),
            device_id_type=MESH,
        )

    def vectors(s):
        if s > 0:
            for move in range(len(stages[s - 1])):
                vector(s - 1, move).wait()
            for move in range(len(stages[s - 1])):
                sums[...] += landing[s - 1 + move]
        if s < 4:
            for move in range(len(stages[s])):
                vector(s, move).start()

    vectors(0)

    def tokens_part(at):
        cols = slice(at, at + 256)
        total = g_low[:, cols].astype(F32)
        for g, w in ((gq, wq), (gk, wk), (gv, wv)):
            total = total + nt(g[...], w[cols, :])
        tokens_grad[:, cols] = total.astype(BF)

    for s in range(1, 4):
        scatter.steps(*TAIL_AFTER[s - 1])
        vectors(s)
        tokens_part((s - 1) * 256)
    scatter.steps(*TAIL_AFTER[3])
    vectors(4)
    for c in range(3):
        for h, half in enumerate("AB"):
            cols = slice(c * 256 + h * 128, c * 256 + h * 128 + 128)
            value = scatter.own(f"h{c}{half}")
            for i, share in enumerate((share_q, share_k, share_v)):
                share[:, cols] = value[i * ROWS : (i + 1) * ROWS]
            share_u[:, cols] = scatter.own(f"u{c}{half}")
    for h, half in enumerate("AB"):
        share_o[:, h * 384 : h * 384 + 384] = scatter.own("o" + half)
    scatter.drain()


TAIL_STEPS = (("u00", "u10"),)
TAIL_BETWEEN = {
    (0, 0): ("u01", "u20"), (0, 1): ("o0", "u11"), (0, 3): ("u02",),
    (1, 0): ("u12", "u21"), (1, 2): ("u03", "o1"),
    (2, 0): ("u22", "u13", "h01"), (2, 2): ("u04", "o2"), (3, 0): ("u23", "h02", "u14"),
    (3, 2): ("o3", "u24"), (4, 0): ("h03", "h11", "o4"), (4, 2): ("h12",), (5, 0): ("h04", "h13"),
    (5, 2): ("h14",),
}
TAIL_AFTER = (("h21",), ("h22",), ("h23",), ("h24",))


def heads_back(lanes, late, q, k, v, o, rd, gm, x, g_low, wq, wk, wv, col, row, sums):
    anywhere = pl.BlockSpec(memory_space=pl.ANY)
    vmem = pl.BlockSpec(memory_space=pltpu.VMEM)
    shape = jax.ShapeDtypeStruct
    return pl.pallas_call(
        lambda *refs: heads_back_kernel(lanes, *refs),
        out_shape=(
            shape((T, D), BF),
            *[shape((ROWS, D), F32)] * 4,
            shape((4 * ROWS, D), F32),
            shape((16, D), F32),
        ),
        in_specs=[anywhere] * len(late) + [vmem] * 14,
        out_specs=(vmem,) * 7,
        scratch_shapes=[
            pltpu.VMEM((T, T), BF),
            *[pltpu.VMEM((T, D), BF)] * 3,
            *[pltpu.VMEM((T, 128), BF)] * 9,
            pltpu.VMEM((T, 128), F32),
            pltpu.VMEM((6, 16, D), F32),
            pltpu.SemaphoreType.DMA((6,)),
            pltpu.SemaphoreType.DMA((6,)),
            pltpu.SemaphoreType.DMA((len(late),)),
            *scatter_scratch(TAIL_PARTS),
        ],
        compiler_params=pltpu.CompilerParams(
            collective_id=5, has_side_effects=True, vmem_limit_bytes=61 * MIB
        ),
        name="heads_back",
    )(*late, q, k, v, o, rd, gm, x, g_low, wq, wk, wv, col, row, sums)


def geometry(lengths, count):
    number = lengths.shape[0]
    order = jnp.arange(number, dtype=jnp.int32)
    upto = order[:, None] <= order[None, :]
    ends = jnp.sum(jnp.where(upto, lengths[:, None], 0), axis=0)
    starts = ends - lengths
    places = jnp.arange(count, dtype=jnp.int32)
    segment = jnp.sum((places[:, None] >= ends[None, :]).astype(jnp.int32), axis=1)
    onehot = segment[:, None] == order[None, :]
    begin = jnp.sum(jnp.where(onehot, starts[None, :], 0), axis=1)
    total = jnp.sum(jnp.where(onehot, lengths[None, :], 0), axis=1)
    angle = 0.5 * math.pi * (places - begin).astype(F32) / total.astype(F32)
    return segment, jnp.cos(angle), jnp.sin(angle)


def group_gather(x, lanes):
    if lanes > 1:
        x = lax.all_gather(x, "shard", axis=0, tiled=True)
    if lanes > 2:
        size = lanes // 2
        count = lax.axis_size("dp")
        parts = [list(range(i, i + size)) for i in range(0, count, size)]
        x = lax.all_gather(x, "dp", axis=0, tiled=True, axis_index_groups=parts)
    return x


def group_scatter(x, lanes):
    if lanes > 2:
        size = lanes // 2
        count = lax.axis_size("dp")
        parts = [list(range(i, i + size)) for i in range(0, count, size)]
        x = lax.psum_scatter(
            x, "dp", scatter_dimension=0, tiled=True, axis_index_groups=parts
        )
    if lanes > 1:
        x = lax.psum_scatter(x, "shard", scatter_dimension=0, tiled=True)
    return x


def body(
    lanes, tokens, seq_lengths,
    query_weight, query_bias, key_weight, key_bias, value_weight, value_bias,
    output_weight, output_bias, norm_gain, norm_shift, inner_weight, inner_bias,
    outer_weight, outer_bias, final_gain, final_shift, cotangent,
):
    segment, cosine, sine = geometry(seq_lengths[0], T)
    weights = [
        group_gather(w, lanes)
        for w in (
            query_weight, key_weight, value_weight, output_weight, inner_weight, outer_weight,
        )
    ]
    vectors = [
        group_gather(v, lanes).reshape(-1, ROWS)
        for v in (
            query_bias, key_bias, value_bias, output_bias, norm_gain, norm_shift,
            outer_bias, final_gain, final_shift,
        )
    ]
    small = jnp.pad(jnp.concatenate(vectors, axis=0), ((0, 0), (0, 128 - ROWS)))
    inside = group_gather(inner_bias, lanes).reshape(1, 4 * ROWS)
    inside = jnp.pad(inside, ((0, 6), (0, 128 - 4 * ROWS)))
    small = jnp.concatenate([small, inside], axis=0)
    place = jnp.stack([cosine, sine, segment.astype(F32)])
    col = jnp.pad(place.T, ((0, 0), (0, 125)))
    row = jnp.pad(place, ((0, 5), (0, 0)))
    outs = forward(lanes, [small] + weights, tokens, col, row, cotangent)
    w_query, w_key, w_value, w_output, w_inner, w_outer = (
        g.reshape(-1, g.shape[-1]) for g in outs[:6]
    )
    (
        query, key, value, mixed, inverse, mixed_low, hat, rstd, normed_low,
        inner, result, g_second, vec, sums,
    ) = outs[6:]
    *late, g_low, g_mixed, sums, share_i = inner_back(
        lanes, g_second, inner, w_outer, normed_low, w_inner, hat, rstd, vec, mixed_low,
        w_output, jnp.concatenate([jnp.zeros((6, D), F32), sums[:3], jnp.zeros((7, D), F32)]),
    )
    tokens_grad, share_q, share_k, share_v, share_o, share_u, sums = heads_back(
        lanes, late, query, key, value, mixed, inverse, g_mixed, tokens, g_low,
        w_query, w_key, w_value, col, row, sums,
    )
    group = (lax.axis_index("dp") * 2 + lax.axis_index("shard")) // lanes
    mine = lax.dynamic_slice(sums, (0, group * ROWS), (9, ROWS))
    vec = [group_scatter(mine[i], lanes) for i in range(9)]
    mine = lax.dynamic_slice(sums[9:13].reshape(FF), (group * 4 * ROWS,), (4 * ROWS,))
    inner_bias_grad = group_scatter(mine, lanes)
    mat = [
        group_scatter(s, lanes)
        for s in (share_q, share_k, share_v, share_o, share_i, share_u)
    ]
    return (
        result, tokens_grad,
        mat[0], vec[0], mat[1], vec[1], mat[2], vec[2], mat[3], vec[3],
        vec[4], vec[5], mat[4], inner_bias_grad, mat[5], vec[6], vec[7], vec[8],
    )


def solution(mesh):
    lanes = mesh.shape["dp"] * mesh.shape["shard"] // GROUPS
    rows, flat = P(AXES, None), P(AXES)
    return jax.shard_map(
        lambda *args: body(lanes, *args),
        mesh=mesh,
        in_specs=(rows, rows) + (rows, flat) * 4 + (flat, flat) + (rows, flat) * 2 + (flat, flat, rows),
        out_specs=(rows, rows) + (rows, flat) * 4 + (flat, flat) + (rows, flat) * 2 + (flat, flat),
        check_vma=False,
    )
```

```python
import math

import jax
import jax.numpy as jnp
from jax import lax
from jax.experimental import pallas as pl
from jax.experimental.pallas import tpu as pltpu
from jax.sharding import PartitionSpec as P

BF = jnp.bfloat16
F32 = jnp.float32
MESH = pl.DeviceIdType.MESH
AXES = ("dp", "shard")
D = 768
FF = 3072
HD = 64
T = 1024
B = 256
NB = T // B
GROUPS = 32
ROWS = D // GROUPS
MIB = 2**20


def nt(a, b):
    return lax.dot_general(a, b, (((1,), (1,)), ((), ())), preferred_element_type=F32)


def nn(a, b):
    return jnp.dot(a, b, preferred_element_type=F32)


def tn(a, b):
    return lax.dot_general(a, b, (((0,), (0,)), ((), ())), preferred_element_type=F32)


def softplus(x):
    return jnp.maximum(x, 0.0) + jnp.log1p(jnp.exp(-jnp.abs(x)))


CORE = 3
LINE = ((0,), (1,), (0, 1))
GATHER_ORDER = {
    "A": (LINE, ((2,),), ((4,),)),
    "B": (LINE, ((4,),), ((2,),)),
    "E": (((4,),), LINE, ((2,),)),
    "F": (((2,),), LINE, ((4,),)),
}
ARRAYS = "shoiu"
SHAPES = {
    "s": (16, 128),
    "h": (3, ROWS, D),
    "o": (ROWS, D),
    "i": (ROWS, FF),
    "u": (FF // GROUPS, D),
}
S, O, H0, H1, H2, U0, U1, U2, I0, I1, I2, I3 = (
    "s o h0 h1".split() + "h2 u0 u1 u2".split() + "i0 i1 i2 i3".split()
)
LOAD = 9
(
    BEFORE, PROJECT, HEADS, OUT, INNER, OUTER, GELU, BACK, NORM, MIXED, AFTER,
) = range(11)
GATHER_TYPES = {
    O: "BFE",
    I0: "FEE",
    I1: "AAB",
    I2: "AEA",
    I3: "BAA",
    U0: "AB",
    U1: "FB",
    U2: "EF",
}
FORWARD_STEPS = {
    (BEFORE, 0): ((S, 0), (H0, 0), (I0, 0),),
    (BEFORE, 1): ((H1, 0),),
    (BEFORE, 2): ((S, 1), (H0, 1), (H2, 0), (I3, 0),),
    (BEFORE, 3): ((O, 0), (I2, 0), (U2, 0),),
    (BEFORE, 4): ((H1, 1),),
    (BEFORE, 5): ((S, 2), (H0, 2), (H2, 1), (I3, 1), (U1, 0),),
    (BEFORE, 6): ((S, 3), (H0, 3), (H1, 2), (O, 1), (I1, 0),),
    (BEFORE, 7): ((I3, 2), (S, 4), (H0, 4),),
    (PROJECT, 0): ((I2, 1),),
    (HEADS, 0, 0): ((H2, 2),),
    (HEADS, 0, 3): ((O, 2),),
    (HEADS, 1, 0): ((H1, 3), (I0, 1),),
    (HEADS, 1, 2): ((U0, 0),),
    (HEADS, 1, 3): ((I1, 1), (I2, 2), (H1, 4),),
    (HEADS, 2, 0): ((U1, 1),),
    (HEADS, 2, 2): ((H2, 3),),
    (HEADS, 3, 0): ((O, 3),),
    (HEADS, 3, 1): ((I0, 2),),
    (HEADS, 3, 2): ((U2, 1),),
    (HEADS, 3, 3): ((I1, 2), (H2, 4),),
    (PROJECT, 2): ((I2, 3),),
    (HEADS, 4, 1): ((I3, 3), (U0, 1),),
    (HEADS, 4, 2): ((I0, 3),),
    (HEADS, 5, 1): ((O, 4), (O, LOAD),),
    (HEADS, 5, 2): ((U1, 2), (I0, 4), (I0, LOAD),),
    (HEADS, 5, 3): ((I1, 3),),
    (OUT, 1): ((U0, 2),),
    (INNER, 0, 0): ((I1, 4), (I1, LOAD),),
    (INNER, 1, 0): ((U2, 2), (I2, 4), (I2, LOAD),),
    (INNER, 1, 1): ((U1, 3),),
    (INNER, 2, 0): ((U0, 3), (I3, 4), (I3, LOAD),),
    (INNER, 3, 0): ((U0, 4), (U0, LOAD),),
    (INNER, 3, 1): ((U2, 3),),
    (INNER, 3, 2): ((U1, 4), (U1, LOAD),),
    (OUTER, 0, 1): ((U2, 4), (U2, LOAD),),
}
INNER_STEPS = {
    (INNER, 1, 0): ((I0, 1),),
    (INNER, 2, 0): ((I0, 2),),
    (BACK, 2, 0): ((I1, 1),),
    (GELU, 3, 0): ((I2, 1),),
    (INNER, 3, 1): ((I0, 3),),
    (BACK, 3, 0): ((I1, 2), (I2, 2),),
    (BACK, 3, 2): ((I3, 1),),
    (NORM, 1): ((I1, 3),),
    (MIXED, 1): ((I2, 3), (I3, 2),),
    (OUTER, 0, 1): ((I0, 4), (I3, 3),),
    (OUTER, 2, 1): ((I2, 4),),
    (OUTER, 2, 3): ((I1, 4), (I3, 4),),
}
TAIL_STEPS = {
    (BEFORE, 0): ((O, 0),),
    (HEADS, 0, 0): ((U2, 0), (O, 1),),
    (HEADS, 0, 1): ((U0, 0),),
    (HEADS, 1, 0): ((U1, 0),),
    (HEADS, 1, 2): ((U2, 1),),
    (HEADS, 1, 3): ((U1, 1), (O, 2),),
    (PROJECT, 0): ((U0, 1),),
    (PROJECT, 1): ((U1, 2), (U2, 2),),
    (HEADS, 4, 0): ((H0, 1),),
    (HEADS, 4, 2): ((U1, 3),),
    (HEADS, 4, 3): ((H1, 1),),
    (HEADS, 5, 0): ((U2, 3), (O, 3), (H0, 2),),
    (HEADS, 5, 1): ((H1, 2),),
    (PROJECT, 2): ((U0, 2), (H0, 3), (H1, 3), (H2, 1),),
    (AFTER, 1): ((U0, 3), (H2, 2),),
    (AFTER, 2): ((U2, 4), (O, 4), (H0, 4), (H2, 3),),
    (AFTER, 3): ((H1, 4),),
    (AFTER, 4): ((U0, 4), (U1, 4), (H2, 4),),
}
GATHER_PARTS = {"s": ("s", (("A", 0, 128),))}
for c in range(3):
    GATHER_PARTS[f"h{c}"] = ("h", (("A", c * 256, 128), ("B", c * 256 + 128, 128)))
    GATHER_PARTS[f"u{c}"] = (
        "u",
        tuple((t, c * 256 + p * 128, 128) for p, t in enumerate(GATHER_TYPES[f"u{c}"])),
    )
for name in ("o", "i0", "i1", "i2", "i3"):
    first = int(name[1:] or 0) * D
    GATHER_PARTS[name] = (
        name[0],
        tuple((t, first + p * 256, 256) for p, t in enumerate(GATHER_TYPES[name])),
    )
GATHER_JOBS = {}
for name, (_, parts) in GATHER_PARTS.items():
    for part, (kind, _, _) in enumerate(parts):
        for s, moves in enumerate(GATHER_ORDER[kind] + (((CORE,), (CORE,)),)):
            for move in range(len(moves)):
                GATHER_JOBS[name, part, s, move] = len(GATHER_JOBS)


class Where:
    def __init__(self, lanes):
        self.dp = lax.axis_index("dp")
        self.shard = lax.axis_index("shard")
        self.lanes = lanes
        group = (self.dp * 2 + self.shard) // lanes
        self.bits = [lax.rem(group // (16 >> e), 2) for e in range(5)]

    def partner(self, *flips):
        dp, shard = self.dp, self.shard
        for e in flips:
            step = (16 >> e) * self.lanes
            if step == 1:
                shard = 1 - shard
            else:
                step = step // 2
                dp = dp + step - 2 * step * self.bits[e]
        return (dp, shard)

    def barrier(self, moves=((0,), (1,), (0, 1), (2,), (3,), (4,))):
        bar = pltpu.get_barrier_semaphore()
        for move in moves:
            pl.semaphore_signal(
                bar, inc=1, device_id=self.partner(*move), device_id_type=MESH
            )
        pl.semaphore_wait(bar, len(moves))


class Gather:
    def __init__(self, where, shards, bufs, send, recv, loc):
        self.where = where
        self.shards = shards
        self.bufs = bufs
        self.send = send
        self.recv = recv
        self.loc = loc

    def view(self, a, full, start, size, flip=()):
        index = []
        for e in range(5):
            bit = self.where.bits[e]
            index.append(slice(None) if e in full else (1 - bit if e in flip else bit))
        rest = (slice(None),) * (len(SHAPES[a]) - 1) + (pl.ds(start, size),)
        return self.bufs[a].at[tuple(index) + rest]

    def local(self, a):
        return pltpu.make_async_copy(
            self.shards[a], self.view(a, (), 0, SHAPES[a][-1]), self.loc.at[ARRAYS.index(a)]
        )

    def job(self, name, part, s, move):
        a, parts = GATHER_PARTS[name]
        kind, start, size = parts[part]
        order = GATHER_ORDER[kind]
        done = [e for stage in order[: min(s, len(order) - 1)] for m in stage for e in m]
        if s < len(order):
            flips = order[s][move]
            dst = self.view(a, done, start, size)
        else:
            flips = (CORE,)
            dst = self.view(a, done, start, size, flip=order[-1][0] if move else ())
        src = dst
        if s == 0:
            rest = (slice(None),) * (len(SHAPES[a]) - 1) + (pl.ds(start, size),)
            src = self.shards[a].at[rest]
        n = GATHER_JOBS[name, part, s, move]
        return pltpu.make_async_remote_copy(
            src_ref=src,
            dst_ref=dst,
            send_sem=self.send.at[n],
            recv_sem=self.recv.at[n],
            device_id=self.where.partner(*flips),
            device_id_type=MESH,
        )

    def step(self, name, s):
        for part, (kind, _, _) in enumerate(GATHER_PARTS[name][1]):
            order = GATHER_ORDER[kind]
            last = len(order)
            if 0 < s <= last:
                for move in range(len(order[s - 1])):
                    self.job(name, part, s - 1, move).wait_recv()
            if s < last:
                for move in range(len(order[s])):
                    self.job(name, part, s, move).start()
            if s == last - 1:
                self.job(name, part, last, 0).start()
            if s == last:
                self.job(name, part, last, 1).start()
            if s == last + 1:
                self.job(name, part, last, 0).wait_recv()
                self.job(name, part, last, 1).wait_recv()

    def drain(self):
        for key in GATHER_JOBS:
            self.job(*key).wait_send()


SCATTER_ORDER = {
    "A": (((CORE,),), ((4,),), ((2,),), LINE),
    "B": (((CORE,),), ((2,),), ((4,),), LINE),
}
INNER_PARTS = {f"i{m}{h}": (h, ROWS, 384) for m in range(4) for h in "AB"}
LATE_PARTS = {f"u{c}{h}": (h, 4 * ROWS, 128) for c in range(3) for h in "AB"}
LATE_PARTS.update({f"o{h}": (h, ROWS, 384) for h in "AB"})
HEAD_PARTS = {f"h{c}{h}": (h, 3 * ROWS + 8, 128) for c in range(3) for h in "AB"}
TAIL_PARTS = {**LATE_PARTS, **HEAD_PARTS}


def scatter_jobs(parts):
    jobs = {}
    for name, (kind, _, _) in parts.items():
        for s, moves in enumerate(SCATTER_ORDER[kind]):
            for move in range(len(moves)):
                jobs[name, s, move] = len(jobs)
    return jobs


def scatter_scratch(parts):
    scratch = []
    for _, rows, size in parts.values():
        scratch += [
            pltpu.VMEM(dims + (rows, size), BF)
            for dims in ((2,) * 5, (2,) * 4, (2,) * 3, (2,) * 2, (3,))
        ]
    jobs = len(scatter_jobs(parts))
    return scratch + [pltpu.SemaphoreType.DMA((jobs,)), pltpu.SemaphoreType.DMA((jobs,))]


def scatter_count(parts):
    return 5 * len(parts) + 2


class Scatter:
    def __init__(self, where, parts, refs):
        self.where = where
        self.parts = parts
        self.grads = {name: refs[5 * i] for i, name in enumerate(parts)}
        self.landing = {name: refs[5 * i + 1 : 5 * i + 5] for i, name in enumerate(parts)}
        self.send, self.recv = refs[5 * len(parts) :]
        self.jobs = scatter_jobs(parts)

    def index(self, name, s, flips):
        order = SCATTER_ORDER[self.parts[name][0]]
        moved = [e for stage in order[: s + 1] for m in stage for e in m]
        index = []
        for e in range(5):
            bit = self.where.bits[e]
            index.append((1 - bit if e in flips else bit) if e in moved else slice(None))
        return tuple(index)

    def job(self, name, s, move):
        flips = SCATTER_ORDER[self.parts[name][0]][s][move]
        n = self.jobs[name, s, move]
        landing = self.landing[name][s]
        return pltpu.make_async_remote_copy(
            src_ref=self.grads[name].at[self.index(name, s, flips)],
            dst_ref=landing.at[move] if s == 3 else landing,
            send_sem=self.send.at[n],
            recv_sem=self.recv.at[n],
            device_id=self.where.partner(*flips),
            device_id_type=MESH,
        )

    def add(self, name, s):
        index = self.index(name, s, ())
        grads, landing = self.grads[name], self.landing[name][s]
        if s == 3:
            total = grads[index].astype(F32)
            for move in range(3):
                total = total + landing[move].astype(F32)
            grads[index] = total.astype(BF)
            return
        free = [e for e in range(5) if isinstance(index[e], slice)]

        def one(t, _):
            bits = [lax.rem(t // (1 << (3 - s - k)), 2) for k in range(4 - s)]
            at = list(index)
            for k, e in enumerate(free):
                at[e] = bits[k]
            grads[tuple(at)] = grads[tuple(at)] + landing[tuple(bits)]
            return 0

        lax.fori_loop(0, 1 << (4 - s), one, 0)

    def step(self, name, s):
        for half in "AB":
            part = name + half
            moves = SCATTER_ORDER[half]
            if s > 0:
                for move in range(len(moves[s - 1])):
                    self.job(part, s - 1, move).wait_recv()
                self.add(part, s - 1)
            if s < 4:
                for move in range(len(moves[s])):
                    self.job(part, s, move).start()

    def own(self, part):
        return self.grads[part][tuple(self.where.bits)].astype(F32)

    def drain(self):
        for key in self.jobs:
            self.job(*key).wait_send()


def spread(dst, value, rows, at):
    dims = len(dst.shape) - 2
    for g in range(1 << dims):
        bits = tuple((g >> (dims - 1 - e)) & 1 for e in range(dims))
        dst[bits + (slice(at, at + rows),)] = value[g * rows : (g + 1) * rows].astype(BF)


def rows_of(t, size):
    return pl.ds(pl.multiple_of(t * size, size), size)


def assemble(w, staged, cols):
    for g in range(GROUPS):
        bits = tuple((g >> (4 - e)) & 1 for e in range(5))
        w[g * ROWS : (g + 1) * ROWS, cols] = staged[bits]


def fill_turn(c_ref, col_ref, row_ref, transposed):
    for i in range(NB):
        for j in range(NB):
            if (j < i) if transposed else (j > i):
                continue
            r, w = slice(i * B, (i + 1) * B), slice(j * B, (j + 1) * B)
            turn = col_ref[r, 0:1] * row_ref[0:1, w] + col_ref[r, 1:2] * row_ref[1:2, w]
            allowed = col_ref[r, 2:3] == row_ref[2:3, w]
            if i == j:
                mine = lax.broadcasted_iota(jnp.int32, (B, B), 0)
                other = lax.broadcasted_iota(jnp.int32, (B, B), 1)
                allowed &= (other >= mine) if transposed else (other <= mine)
            c_ref[r, w] = jnp.where(allowed, turn, 0.0).astype(BF)


def normalize(h):
    center = h - jnp.mean(h, axis=1, keepdims=True)
    rstd = lax.rsqrt(jnp.mean(center * center, axis=1, keepdims=True) + 1e-05)
    return center * rstd, rstd


KEPT = ("q", "k", "v", "o", "rd", "mixed", "hat", "rstd", "low", "inner", "wq", "wk", "wv")


def forward_kernel(lanes, *refs):
    n = len(ARRAYS)
    shards = dict(zip(ARRAYS, refs[:n]))
    x, col, row, cot_in = refs[n : n + 4]
    refs = refs[n + 4 :]
    bufs = dict(zip("oiu", refs[:3]))
    result, g_second, vec, sums = refs[3:7]
    kept_out = refs[7 : 7 + len(KEPT)]
    refs = refs[7 + len(KEPT) :]
    kept = refs[: len(KEPT)]
    q, k, v, o, rd, mixed, hat, rstd, low, inner, *heads = kept
    (
        small, all_h, staged, staged_u, w, c_ref, fq, fk0, fk1, v0, v1, acc, act,
        b_inner, send, recv, loc, load, keep_sem,
    ) = refs[len(KEPT) :]
    bufs["s"], bufs["h"] = small, all_h
    gather = Gather(Where(lanes), shards, bufs, send, recv, loc)
    for a in ARRAYS:
        gather.local(a).start()

    def keep(name):
        i = KEPT.index(name)
        return pltpu.make_async_copy(kept[i], kept_out[i], keep_sem.at[i])

    def loads(name):
        j = int(name[1:] or 0)
        if name[0] == "u":
            src = bufs["u"].at[(slice(None),) * 6 + (pl.ds(j * 256, 256),)]
            return [pltpu.make_async_copy(src, staged_u.at[j % 2], load.at[j % 2])]
        at = 0 if name == "o" else (j + 1) % 2
        src = bufs[name[0]].at[(slice(None),) * 6 + (pl.ds(j * D, D),)]
        return [pltpu.make_async_copy(src, staged.at[at], load.at[3 + at])]

    def slot(*place):
        for name, what in FORWARD_STEPS.get(place, ()):
            if what == LOAD:
                for copy in loads(name):
                    copy.start()
            else:
                gather.step(name, what)

    def arrived(name):
        for copy in loads(name):
            copy.wait()

    gather.where.barrier()
    slot(BEFORE, 0)
    fill_turn(c_ref, col, row, False)
    for a in ARRAYS:
        gather.local(a).wait()
    for i in range(1, 8):
        slot(BEFORE, i)
    vec[...] = jnp.zeros_like(vec)
    b_inner[...] = jnp.zeros_like(b_inner)
    lane = lax.broadcasted_iota(jnp.int32, (16, 256), 1)
    for g in range(GROUPS):
        bits = tuple((g >> (4 - e)) & 1 for e in range(5))
        mine = small[bits].astype(F32)
        mine = jnp.concatenate([mine, jnp.zeros_like(mine)], axis=1)
        for dst, rows, width in ((vec, slice(0, 16), ROWS), (b_inner, slice(8, 16), 4 * ROWS)):
            at = g * width
            piece = jnp.where(lane < width, mine, 0.0)
            if at % 128:
                piece = pltpu.roll(piece, at % 128, 1)
            at = at // 128 * 128
            dst[:, at : at + 256] += piece[rows]
    for c in range(3):
        cols = slice(c * 256, c * 256 + 256)
        for i, out in enumerate((q, k, v)):
            assemble(heads[i], all_h.at[:, :, :, :, :, i, :, cols], cols)
            out[:, cols] = (nn(x[...], heads[i][:, cols]) + vec[i : i + 1, cols]).astype(BF)
        slot(PROJECT, c)
        if c == 2:
            for name in ("q", "k", "v", "wq", "wk", "wv"):
                keep(name).start()

        def between(hp, i):
            for at in (2 * c, 2 * c + 1):
                if (HEADS, at, i) in FORWARD_STEPS:
                    pl.when(hp == at)(lambda at=at: slot(HEADS, at, i))

        attend(2 * c, c_ref, q, k, v, o, rd, fq, fk0, fk1, v0, v1, between)
    keep("o").start()
    keep("rd").start()
    arrived("o")
    assemble(w, staged.at[0], slice(0, D))

    def attended(t, _):
        r = rows_of(t, B)
        low_mixed = o[r, :].astype(BF)
        mixed[r, :] = low_mixed
        first = x[r, :].astype(F32) + nn(low_mixed, w[...]) + vec[3:4, :D]
        xhat, spread = normalize(first)
        hat[r, :] = xhat.astype(BF)
        rstd[r, :] = jnp.broadcast_to(spread, (B, 128))
        normed = xhat * vec[4:5, :D] + vec[5:6, :D]
        low[r, :] = normed.astype(BF)
        acc[r, :] = normed + vec[6:7, :D]
        return 0

    lax.fori_loop(0, 2, attended, 0)
    slot(OUT, 0)
    lax.fori_loop(2, 4, attended, 0)
    slot(OUT, 1)
    for name in ("mixed", "hat", "rstd", "low"):
        keep(name).start()
    keep("q").wait()
    cot_copy = pltpu.make_async_copy(cot_in, q, load.at[5])
    cot_copy.start()
    for j in range(4):
        arrived(f"i{j}")
        assemble(w, staged.at[(j + 1) % 2], slice(0, D))
        for n in range(3):
            cols = slice(j * D + n * 256, j * D + n * 256 + 256)
            hidden = nn(low[...], w[:, n * 256 : n * 256 + 256]) + b_inner[1:2, cols]
            inner[:, cols] = hidden.astype(BF)
            act[:, cols] = jax.nn.gelu(hidden).astype(BF)
            slot(INNER, j, n)
    keep("inner").start()
    for c in range(3):
        cols = slice(c * 256, c * 256 + 256)
        arrived(f"u{c}")
        for half in range(2):
            r = slice(half * 512, half * 512 + 512)
            acc[r, cols] += nn(act[r, :], staged_u[c % 2].reshape(FF, 256))
            slot(OUTER, c, half)
    sums[...] = jnp.zeros_like(sums)
    cot_copy.wait()

    def final(t, _):
        r = rows_of(t, 128)
        xhat, spread = normalize(acc[r, :])
        gain = vec[7:8, :D]
        result[r, :] = (xhat * gain + vec[8:9, :D]).astype(BF)
        back = q[r, :].astype(F32)
        scaled = back * gain
        g = spread * (
            scaled
            - jnp.mean(scaled, axis=1, keepdims=True)
            - xhat * jnp.mean(scaled * xhat, axis=1, keepdims=True)
        )
        g_second[r, :] = g
        sums[0:1, :] += jnp.sum(g.astype(BF).astype(F32), axis=0, keepdims=True)
        sums[1:2, :] += jnp.sum(back * xhat, axis=0, keepdims=True)
        sums[2:3, :] += jnp.sum(back, axis=0, keepdims=True)
        return 0

    lax.fori_loop(0, T // 128, final, 0)
    for name in KEPT[1:]:
        keep(name).wait()
    gather.drain()


def forward(lanes, arrays, x, col, row, cot):
    anywhere = pl.BlockSpec(memory_space=pl.ANY)
    vmem = pl.BlockSpec(memory_space=pltpu.VMEM)
    jobs = len(GATHER_JOBS)
    rows, wide = ((T, D), BF), ((T, D), F32)
    kept = [
        rows, rows, rows, wide, rows, rows, rows, ((T, 128), F32), rows, ((T, FF), BF),
        ((D, D), BF), ((D, D), BF), ((D, D), BF),
    ]
    outs = [((2,) * 5 + SHAPES[a], BF) for a in "oiu"]
    outs += [rows, wide, ((16, D + 128), F32), ((8, D), F32)] + kept
    return pl.pallas_call(
        lambda *refs: forward_kernel(lanes, *refs),
        out_shape=tuple(jax.ShapeDtypeStruct(*out) for out in outs),
        in_specs=[vmem] * (len(ARRAYS) + 3) + [anywhere],
        out_specs=(anywhere,) * 3 + (vmem,) * 4 + (anywhere,) * len(kept),
        scratch_shapes=[
            *[pltpu.VMEM(*one) for one in kept],
            pltpu.VMEM((2,) * 5 + SHAPES["s"], BF),
            pltpu.VMEM((2,) * 5 + SHAPES["h"], BF),
            pltpu.VMEM((2,) + (2,) * 5 + (ROWS, D), BF),
            pltpu.VMEM((2,) + (2,) * 5 + (FF // GROUPS, 256), BF),
            pltpu.VMEM((D, D), BF),
            pltpu.VMEM((T, T), BF),
            *[pltpu.VMEM((T, 128), BF)] * 5,
            pltpu.VMEM((T, D), F32),
            pltpu.VMEM((T, FF), BF),
            pltpu.VMEM((8, FF + 128), F32),
            pltpu.SemaphoreType.DMA((jobs,)),
            pltpu.SemaphoreType.DMA((jobs,)),
            pltpu.SemaphoreType.DMA((len(ARRAYS),)),
            pltpu.SemaphoreType.DMA((6,)),
            pltpu.SemaphoreType.DMA((len(kept),)),
        ],
        compiler_params=pltpu.CompilerParams(
            collective_id=3, has_side_effects=True, vmem_limit_bytes=61 * MIB
        ),
        name="forward",
    )(*arrays, x, col, row, cot)


def attend(first, c_ref, q_ref, k_ref, v_ref, o_ref, rd_ref, fq, fk0, fk1, v0, v1, between):
    left = lax.broadcasted_iota(jnp.int32, (T, 128), 1) < 64
    left_block = lax.broadcasted_iota(jnp.int32, (B, 128), 1) < 64

    def pair(hp, _):
        sl = pl.ds(pl.multiple_of(hp * 128, 128), 128)
        fq[...] = softplus(q_ref[:, sl].astype(F32)).astype(BF)
        sk = softplus(k_ref[:, sl].astype(F32))
        fk0[...] = jnp.where(left, sk, 0.0).astype(BF)
        fk1[...] = jnp.where(left, 0.0, sk).astype(BF)
        vv = v_ref[:, sl].astype(F32)
        v0[...] = jnp.where(left, vv, 1.0).astype(BF)
        v1[...] = jnp.where(left, 1.0, vv).astype(BF)
        for i in range(NB):
            r, w = slice(i * B, (i + 1) * B), slice(0, (i + 1) * B)
            sums = []
            for fk, vx in ((fk0, v0), (fk1, v1)):
                weight = nt(fq[r], fk[w]).astype(BF) * c_ref[r, w]
                sums.append(nn(weight, vx[w]))
            numer = jnp.where(left_block, sums[0], sums[1])
            denom = pltpu.roll(jnp.where(left_block, sums[1], sums[0]), 64, 1)
            rd = 1.0 / denom
            o_ref[r, sl] = numer * rd
            rd_ref[r, sl] = rd.astype(BF)
            between(hp, i)
        return 0

    lax.fori_loop(first, first + 2, pair, 0)


def inner_back_kernel(lanes, *refs):
    given = refs[:9]
    vec, sums_in = refs[9:11]
    late_out = dict(zip(LATE_PARTS, refs[11:19]))
    g_low_out, g_mixed_out, sums, shares = refs[19:23]
    held = refs[23:32]
    gn, hid, wu, lo, wi, hat, rstd, mixed, wo = held
    act = refs[32]
    late = dict(zip(LATE_PARTS, refs[33:41]))
    gb, g_low, g_mixed, load_sem, late_sem = refs[41:46]
    scatter = Scatter(Where(lanes), INNER_PARTS, refs[46:])

    def load(i):
        return pltpu.make_async_copy(given[i], held[i], load_sem.at[i])

    def keep(name):
        if name in late:
            i = list(late).index(name)
            return pltpu.make_async_copy(late[name], late_out[name], late_sem.at[i])
        src, dst, i = (g_low, g_low_out, 8) if name == "low" else (g_mixed, g_mixed_out, 9)
        return pltpu.make_async_copy(src, dst, late_sem.at[i])

    def slot(*place):
        for name, s in INNER_STEPS.get(place, ()):
            scatter.step(name, s)

    for i in range(9):
        load(i).start()
    scatter.where.barrier()
    sums[...] = sums_in[...]
    load(0).wait()
    gb[...] = gn[...].astype(BF)
    load(1).wait()
    load(2).wait()
    c0 = math.sqrt(2.0 / math.pi)
    for m in range(4):
        for n in range(3):
            at = n * 256
            cols = slice(m * D + at, m * D + at + 256)
            back = nt(gb[...], wu[cols, :])
            h = hid[:, cols].astype(F32)
            square = h * h
            t = jnp.tanh(c0 * h * (1.0 + 0.044715 * square))
            half = 0.5 + 0.5 * t
            act[:, cols] = (h * half).astype(BF)
            slope = half + 0.5 * h * (1.0 - t * t) * (c0 * (1.0 + 3 * 0.044715 * square))
            g = (back * slope).astype(BF)
            hid[:, cols] = g
            sums[9 + m : 10 + m, at : at + 256] = jnp.sum(
                g.astype(F32), axis=0, keepdims=True
            )
            slot(GELU, m, n)
        if m == 0:
            load(3).wait()
            load(4).wait()
        for h, half in enumerate("AB"):
            cols = slice(m * D + h * 384, m * D + h * 384 + 384)
            spread(scatter.grads[f"i{m}{half}"], tn(lo[...], hid[:, cols]), ROWS, 0)
            if h:
                scatter.step(f"i{m}", 0)
            slot(INNER, m, h)
        for n in range(3):
            at = n * 256
            gn[:, at : at + 256] += nt(
                hid[:, m * D : (m + 1) * D], wi[at : at + 256, m * D : (m + 1) * D]
            )
            slot(BACK, m, n)
    for i in range(5, 9):
        load(i).wait()

    def first_back(t, _):
        r = rows_of(t, 128)
        g = gn[r, :]
        xhat = hat[r, :].astype(F32)
        sums[4:5, :] += jnp.sum(g * xhat, axis=0, keepdims=True)
        sums[5:6, :] += jnp.sum(g, axis=0, keepdims=True)
        scaled = g * vec[4:5, :D]
        g_first = rstd[r, 0:1] * (
            scaled
            - jnp.mean(scaled, axis=1, keepdims=True)
            - xhat * jnp.mean(scaled * xhat, axis=1, keepdims=True)
        )
        g_attended = g_first.astype(BF)
        g_low[r, :] = g_attended
        sums[3:4, :] += jnp.sum(g_attended.astype(F32), axis=0, keepdims=True)
        return 0

    lax.fori_loop(0, 4, first_back, 0)
    slot(NORM, 0)
    lax.fori_loop(4, 8, first_back, 0)
    slot(NORM, 1)
    keep("low").start()
    for n in range(3):
        at = n * 256
        g_mixed[:, at : at + 256] = nt(g_low[...], wo[at : at + 256, :]).astype(BF)
        slot(MIXED, n)
    keep("mixed").start()
    for h, half in enumerate("AB"):
        spread(late["o" + half], tn(mixed[...], g_low[:, h * 384 : h * 384 + 384]), ROWS, 0)
        keep("o" + half).start()
        slot(OUT, h)
    for c in range(3):
        for m in range(4):
            value = tn(act[:, m * D : (m + 1) * D], gb[:, c * 256 : c * 256 + 256])
            for h, half in enumerate("AB"):
                spread(
                    late[f"u{c}{half}"].at[m // 2, m % 2],
                    value[:, h * 128 : h * 128 + 128],
                    4 * ROWS,
                    0,
                )
            slot(OUTER, c, m)
        for half in "AB":
            keep(f"u{c}{half}").start()
    for m in range(4):
        shares[:, m * D : m * D + 384] = scatter.own(f"i{m}A")
        shares[:, m * D + 384 : (m + 1) * D] = scatter.own(f"i{m}B")
    for name in (*late, "low", "mixed"):
        keep(name).wait()
    scatter.drain()


def inner_back(lanes, given, vec, sums):
    anywhere = pl.BlockSpec(memory_space=pl.ANY)
    vmem = pl.BlockSpec(memory_space=pltpu.VMEM)
    rows = ((T, D), BF)
    late = [((2,) * 5 + p[1:], BF) for p in LATE_PARTS.values()]
    outs = late + [rows, rows, ((16, D), F32), ((ROWS, FF), F32)]
    return pl.pallas_call(
        lambda *refs: inner_back_kernel(lanes, *refs),
        out_shape=tuple(jax.ShapeDtypeStruct(*out) for out in outs),
        in_specs=[anywhere] * 9 + [vmem] * 2,
        out_specs=(anywhere,) * (len(late) + 2) + (vmem,) * 2,
        scratch_shapes=[
            *[pltpu.VMEM(g.shape, g.dtype) for g in given],
            pltpu.VMEM((T, FF), BF),
            *[pltpu.VMEM(*one) for one in late],
            *[pltpu.VMEM(*rows)] * 3,
            pltpu.SemaphoreType.DMA((9,)),
            pltpu.SemaphoreType.DMA((len(late) + 2,)),
            *scatter_scratch(INNER_PARTS),
        ],
        compiler_params=pltpu.CompilerParams(
            collective_id=4, has_side_effects=True, vmem_limit_bytes=61 * MIB
        ),
        name="inner_back",
    )(*given, vec, sums)


def heads_back_kernel(lanes, *refs):
    late = dict(zip(LATE_PARTS, refs[:8]))
    given = refs[8:19]
    col, row, sums_in = refs[19:22]
    tokens_grad, share_q, share_k, share_v, share_o, share_u, total, biases = refs[22:30]
    held = refs[30:41]
    q, k, v, o, rd, gm, x, g_low, wq, wk, wv = held
    (
        ct, gq, gk, gv, fq, fk0, fk1, v0, v1, g0, g1, e0, e1, aq,
        landing, vec_send, vec_recv, load_sem, late_sem, pair_sem, sums,
    ) = refs[41:62]
    scatter = Scatter(Where(lanes), TAIL_PARTS, refs[62:])
    sums[...] = jnp.zeros_like(sums)
    where = scatter.where

    def pair_load(i, hp):
        sl = pl.ds(pl.multiple_of(hp * 128, 128), 128)
        return pltpu.make_async_copy(
            given[i].at[:, sl], held[i].at[:, sl], pair_sem.at[i, hp]
        )

    def whole_load(i):
        return pltpu.make_async_copy(given[i], held[i], load_sem.at[i])

    def slot(*place):
        for name, s in TAIL_STEPS.get(place, ()):
            scatter.step(name, s)

    def load(name):
        return pltpu.make_async_copy(
            late[name], scatter.grads[name], late_sem.at[list(late).index(name)]
        )

    def first_loads(hp, _):
        for i in range(6):
            pair_load(i, hp).start()
        return 0

    first_loads(0, 0)
    for name in late:
        load(name).start()
    lax.fori_loop(1, 6, first_loads, 0)
    for i in range(6, 11):
        whole_load(i).start()
    where.barrier()
    fill_turn(ct, col, row, True)
    for name in late:
        load(name).wait()
    slot(BEFORE, 0)
    lane = lax.broadcasted_iota(jnp.int32, (T, 128), 1)
    left = lane < 64
    left_block = lax.broadcasted_iota(jnp.int32, (B, 128), 1) < 64

    def pair(hp, _):
        for i in range(6):
            pair_load(i, hp).wait()
        sl = pl.ds(pl.multiple_of(hp * 128, 128), 128)
        fq[...] = softplus(q[:, sl].astype(F32)).astype(BF)
        sk = softplus(k[:, sl].astype(F32))
        fk0[...] = jnp.where(left, sk, 0.0).astype(BF)
        fk1[...] = jnp.where(left, 0.0, sk).astype(BF)
        vv = v[:, sl].astype(F32)
        v0[...] = jnp.where(left, vv, 1.0).astype(BF)
        v1[...] = jnp.where(left, 1.0, vv).astype(BF)
        gn = (gm[:, sl].astype(F32) * rd[:, sl]).astype(BF).astype(F32)
        through = gn * o[:, sl]
        d0 = -jnp.sum(jnp.where(left, through, 0.0), axis=1, keepdims=True)
        d1 = -jnp.sum(jnp.where(left, 0.0, through), axis=1, keepdims=True)
        h0 = d0.astype(BF).astype(F32)
        h1 = d1.astype(BF).astype(F32)
        g0[...] = jnp.where(left, gn, 0.0).astype(BF)
        g1[...] = jnp.where(left, 0.0, gn).astype(BF)
        t0 = jnp.where(lane == 64, h0, jnp.where(lane == 65, d0 - h0, 0.0))
        t1 = jnp.where(lane == 0, h1, jnp.where(lane == 1, d1 - h1, 0.0))
        e0[...] = jnp.where(left, gn, t0).astype(BF)
        e1[...] = jnp.where(left, t1, gn).astype(BF)
        aq[...] = jnp.zeros_like(aq)
        for j in range(NB):
            r, w = slice(j * B, (j + 1) * B), slice(j * B, T)
            keys, values = [], []
            for fk, vx, g, e in ((fk0, v0, g0, e0), (fk1, v1, g1, e1)):
                weight = nt(fk[r], fq[w]).astype(BF) * ct[r, w]
                change = nt(vx[r], e[w]).astype(BF) * ct[r, w]
                values.append(nn(weight, g[w]))
                keys.append(nn(change, fq[w]))
                aq[w] += tn(change, fk[r])
            gv[r, sl] = (values[0] + values[1]).astype(BF)
            back = jnp.where(left_block, keys[0], keys[1])
            gk[r, sl] = (back * jax.nn.sigmoid(k[r, sl].astype(F32))).astype(BF)
            for at in range(6):
                if (HEADS, at, j) in TAIL_STEPS:
                    pl.when(hp == at)(lambda at=at, j=j: slot(HEADS, at, j))
        gq[:, sl] = (aq[...] * jax.nn.sigmoid(q[:, sl].astype(F32))).astype(BF)
        return 0

    stages = SCATTER_ORDER["A"]

    def vector(s, move):
        n = s + move
        return pltpu.make_async_remote_copy(
            src_ref=total,
            dst_ref=landing.at[n],
            send_sem=vec_send.at[n],
            recv_sem=vec_recv.at[n],
            device_id=where.partner(*stages[s][move]),
            device_id_type=MESH,
        )

    def vectors(s):
        if s > 0:
            for move in range(len(stages[s - 1])):
                vector(s - 1, move).wait()
            for move in range(len(stages[s - 1])):
                total[...] += landing[s - 1 + move]
        if s < 4:
            for move in range(len(stages[s])):
                vector(s, move).start()

    total[...] = sums_in[...]
    vectors(0)
    for c in range(3):
        lax.fori_loop(2 * c, 2 * c + 2, pair, 0)
        cols = slice(c * 256, c * 256 + 256)
        vectors(c + 1)
        if c == 0:
            whole_load(6).wait()
        for i, g in enumerate((gq, gk, gv)):
            value = tn(x[...], g[:, cols])
            for h, half in enumerate("AB"):
                spread(
                    scatter.grads[f"h{c}{half}"],
                    value[:, h * 128 : h * 128 + 128],
                    ROWS,
                    i * ROWS,
                )
            sums[i : i + 1, cols] = jnp.sum(g[:, cols].astype(F32), axis=0, keepdims=True)
        for h, half in enumerate("AB"):
            bias_rows = sums[0:8, c * 256 + h * 128 : c * 256 + h * 128 + 128].astype(BF)
            for g in range(GROUPS):
                bits = tuple((g >> (4 - e)) & 1 for e in range(5))
                scatter.grads[f"h{c}{half}"][bits + (slice(3 * ROWS, 3 * ROWS + 8),)] = bias_rows
        scatter.step(f"h{c}", 0)
        slot(PROJECT, c)

    for i in range(7, 11):
        whole_load(i).wait()

    def tokens_part(at):
        cols = slice(at, at + 256)
        total = g_low[:, cols].astype(F32)
        for g, w in ((gq, wq), (gk, wk), (gv, wv)):
            total = total + nt(g[...], w[cols, :])
        tokens_grad[:, cols] = total.astype(BF)

    for s in range(1, 4):
        slot(AFTER, s)
        tokens_part((s - 1) * 256)
    vectors(4)
    slot(AFTER, 4)
    for c in range(3):
        for h, half in enumerate("AB"):
            cols = slice(c * 256 + h * 128, c * 256 + h * 128 + 128)
            value = scatter.own(f"h{c}{half}")
            for i, share in enumerate((share_q, share_k, share_v)):
                share[:, cols] = value[i * ROWS : (i + 1) * ROWS]
            biases[:, cols] = value[3 * ROWS :]
            share_u[:, cols] = scatter.own(f"u{c}{half}")
    for h, half in enumerate("AB"):
        share_o[:, h * 384 : h * 384 + 384] = scatter.own("o" + half)
    scatter.drain()


def heads_back(lanes, late, given, col, row, sums):
    anywhere = pl.BlockSpec(memory_space=pl.ANY)
    vmem = pl.BlockSpec(memory_space=pltpu.VMEM)
    shape = jax.ShapeDtypeStruct
    return pl.pallas_call(
        lambda *refs: heads_back_kernel(lanes, *refs),
        out_shape=(
            shape((T, D), BF),
            *[shape((ROWS, D), F32)] * 4,
            shape((4 * ROWS, D), F32),
            shape((16, D), F32),
            shape((8, D), F32),
        ),
        in_specs=[anywhere] * (len(late) + len(given)) + [vmem] * 3,
        out_specs=(vmem,) * 8,
        scratch_shapes=[
            *[pltpu.VMEM(g.shape, g.dtype) for g in given],
            pltpu.VMEM((T, T), BF),
            *[pltpu.VMEM((T, D), BF)] * 3,
            *[pltpu.VMEM((T, 128), BF)] * 9,
            pltpu.VMEM((T, 128), F32),
            pltpu.VMEM((6, 16, D), F32),
            pltpu.SemaphoreType.DMA((6,)),
            pltpu.SemaphoreType.DMA((6,)),
            pltpu.SemaphoreType.DMA((len(given),)),
            pltpu.SemaphoreType.DMA((len(late),)),
            pltpu.SemaphoreType.DMA((6, 6)),
            pltpu.VMEM((8, D), F32),
            *scatter_scratch(TAIL_PARTS),
        ],
        compiler_params=pltpu.CompilerParams(
            collective_id=5, has_side_effects=True, vmem_limit_bytes=61 * MIB
        ),
        name="heads_back",
    )(*late, *given, col, row, sums)


def hand_over(*arrays):
    def copy(*refs):
        for src, dst in zip(refs[: len(arrays)], refs[len(arrays) :]):
            dst[...] = src[...]

    vmem = pl.BlockSpec(memory_space=pltpu.VMEM)
    return pl.pallas_call(
        copy,
        out_shape=tuple(jax.ShapeDtypeStruct(a.shape, a.dtype) for a in arrays),
        in_specs=[vmem] * len(arrays),
        out_specs=(vmem,) * len(arrays),
        name="hand_over",
    )(*arrays)


def geometry(lengths, count):
    number = lengths.shape[0]
    order = jnp.arange(number, dtype=jnp.int32)
    upto = order[:, None] <= order[None, :]
    ends = jnp.sum(jnp.where(upto, lengths[:, None], 0), axis=0)
    starts = ends - lengths
    places = jnp.arange(count, dtype=jnp.int32)
    segment = jnp.sum((places[:, None] >= ends[None, :]).astype(jnp.int32), axis=1)
    onehot = segment[:, None] == order[None, :]
    begin = jnp.sum(jnp.where(onehot, starts[None, :], 0), axis=1)
    total = jnp.sum(jnp.where(onehot, lengths[None, :], 0), axis=1)
    angle = 0.5 * math.pi * (places - begin).astype(F32) / total.astype(F32)
    return segment, jnp.cos(angle), jnp.sin(angle)


def group_gather(x, lanes):
    if lanes > 1:
        x = lax.all_gather(x, "shard", axis=0, tiled=True)
    if lanes > 2:
        size = lanes // 2
        count = lax.axis_size("dp")
        parts = [list(range(i, i + size)) for i in range(0, count, size)]
        x = lax.all_gather(x, "dp", axis=0, tiled=True, axis_index_groups=parts)
    return x


def group_scatter(x, lanes):
    if lanes > 2:
        size = lanes // 2
        count = lax.axis_size("dp")
        parts = [list(range(i, i + size)) for i in range(0, count, size)]
        x = lax.psum_scatter(
            x, "dp", scatter_dimension=0, tiled=True, axis_index_groups=parts
        )
    if lanes > 1:
        x = lax.psum_scatter(x, "shard", scatter_dimension=0, tiled=True)
    return x


def body(
    lanes, tokens, seq_lengths,
    query_weight, query_bias, key_weight, key_bias, value_weight, value_bias,
    output_weight, output_bias, norm_gain, norm_shift, inner_weight, inner_bias,
    outer_weight, outer_bias, final_gain, final_shift, cotangent,
):
    segment, cosine, sine = geometry(seq_lengths[0], T)
    weights = [
        group_gather(w, lanes)
        for w in (
            query_weight, key_weight, value_weight, output_weight, inner_weight, outer_weight,
        )
    ]
    vectors = [
        group_gather(v, lanes).reshape(-1, ROWS)
        for v in (
            query_bias, key_bias, value_bias, output_bias, norm_gain, norm_shift,
            outer_bias, final_gain, final_shift,
        )
    ]
    small = jnp.pad(jnp.concatenate(vectors, axis=0), ((0, 0), (0, 128 - ROWS)))
    inside = group_gather(inner_bias, lanes).reshape(1, 4 * ROWS)
    inside = jnp.pad(inside, ((0, 6), (0, 128 - 4 * ROWS)))
    small = jnp.concatenate([small, inside], axis=0)
    place = jnp.stack([cosine, sine, segment.astype(F32)])
    col = jnp.pad(place.T, ((0, 0), (0, 125)))
    row = jnp.pad(place, ((0, 5), (0, 0)))
    shards = [small, jnp.stack(weights[:3]), *weights[3:]]
    outs = forward(lanes, shards, tokens, col, row, cotangent)
    w_output, w_inner, w_outer = (g.reshape(-1, g.shape[-1]) for g in outs[:3])
    result, g_second, vec, sums = outs[3:7]
    query, key, value, mixed, inverse, mixed_low, hat, rstd, low, inner, *heads = outs[7:]
    *late, g_low, g_mixed, sums, share_i = inner_back(
        lanes, [g_second, inner, w_outer, low, w_inner, hat, rstd, mixed_low, w_output], vec,
        jnp.concatenate([jnp.zeros((6, D), F32), sums[:3], jnp.zeros((7, D), F32)]),
    )
    *heads, sums, biases = heads_back(
        lanes, late, [query, key, value, mixed, inverse, g_mixed, tokens, g_low, *heads],
        col, row, sums,
    )
    tokens_grad, share_q, share_k, share_v, share_o, share_u, share_i, result = hand_over(
        *heads, share_i, result
    )
    sums = jnp.concatenate([biases[:3], sums[3:]], axis=0)
    group = (lax.axis_index("dp") * 2 + lax.axis_index("shard")) // lanes
    mine = lax.dynamic_slice(sums, (0, group * ROWS), (9, ROWS))
    vec = [group_scatter(mine[i], lanes) for i in range(9)]
    mine = lax.dynamic_slice(sums[9:13].reshape(FF), (group * 4 * ROWS,), (4 * ROWS,))
    inner_bias_grad = group_scatter(mine, lanes)
    mat = [
        group_scatter(s, lanes)
        for s in (share_q, share_k, share_v, share_o, share_i, share_u)
    ]
    return (
        result, tokens_grad,
        mat[0], vec[0], mat[1], vec[1], mat[2], vec[2], mat[3], vec[3],
        vec[4], vec[5], mat[4], inner_bias_grad, mat[5], vec[6], vec[7], vec[8],
    )


def solution(mesh):
    lanes = mesh.shape["dp"] * mesh.shape["shard"] // GROUPS
    rows, flat = P(AXES, None), P(AXES)
    return jax.shard_map(
        lambda *args: body(lanes, *args),
        mesh=mesh,
        in_specs=(rows, rows) + (rows, flat) * 4 + (flat, flat) + (rows, flat) * 2 + (flat, flat, rows),
        out_specs=(rows, rows) + (rows, flat) * 4 + (flat, flat) + (rows, flat) * 2 + (flat, flat),
        check_vma=False,
    )
```

```python
import math

import jax
import jax.numpy as jnp
from jax import lax
from jax.experimental import pallas as pl
from jax.experimental.pallas import tpu as pltpu
from jax.sharding import PartitionSpec as P

BF = jnp.bfloat16
F32 = jnp.float32
MESH = pl.DeviceIdType.MESH
AXES = ("dp", "shard")
D = 768
FF = 3072
HD = 64
T = 1024
B = 256
NB = T // B
GROUPS = 32
ROWS = D // GROUPS
MIB = 2**20


def nt(a, b):
    return lax.dot_general(a, b, (((1,), (1,)), ((), ())), preferred_element_type=F32)


def nn(a, b):
    return jnp.dot(a, b, preferred_element_type=F32)


def tn(a, b):
    return lax.dot_general(a, b, (((0,), (0,)), ((), ())), preferred_element_type=F32)


def softplus(x):
    return jnp.maximum(x, 0.0) + jnp.log1p(jnp.exp(-jnp.abs(x)))


CORE = 3
LINE = ((0,), (1,), (0, 1))
GATHER_ORDER = {
    "A": (LINE, ((2,),), ((4,),)),
    "B": (LINE, ((4,),), ((2,),)),
    "E": (((4,),), LINE, ((2,),)),
    "F": (((2,),), LINE, ((4,),)),
}
ARRAYS = "shoiu"
SHAPES = {
    "s": (16, 128),
    "h": (3, ROWS, D),
    "o": (ROWS, D),
    "i": (ROWS, FF),
    "u": (FF // GROUPS, D),
}
S, O, H0, H1, H2, U0, U1, U2, I0, I1, I2, I3 = (
    "s o h0 h1".split() + "h2 u0 u1 u2".split() + "i0 i1 i2 i3".split()
)
LOAD = 9
(
    BEFORE, PROJECT, HEADS, OUT, INNER, OUTER, GELU, BACK, NORM, MIXED, AFTER,
) = range(11)
GATHER_TYPES = {
    O: "BFE",
    I0: "FEE",
    I1: "AAB",
    I2: "AEA",
    I3: "BAA",
    U0: "AB",
    U1: "FB",
    U2: "EF",
}
FORWARD_STEPS = {
    (BEFORE, 0): ((S, 0), (H0, 0), (I0, 0),),
    (BEFORE, 1): ((H1, 0),),
    (BEFORE, 2): ((S, 1), (H0, 1), (H2, 0), (I3, 0),),
    (BEFORE, 3): ((O, 0), (I2, 0), (U2, 0),),
    (BEFORE, 4): ((H1, 1),),
    (BEFORE, 5): ((S, 2), (H0, 2), (H2, 1), (I3, 1), (U1, 0),),
    (BEFORE, 6): ((S, 3), (H0, 3), (H1, 2), (O, 1), (I1, 0),),
    (BEFORE, 7): ((I3, 2), (S, 4), (H0, 4),),
    (PROJECT, 0): ((I2, 1),),
    (HEADS, 0, 0): ((H2, 2),),
    (HEADS, 0, 3): ((O, 2),),
    (HEADS, 1, 0): ((H1, 3), (I0, 1),),
    (HEADS, 1, 2): ((U0, 0),),
    (HEADS, 1, 3): ((I1, 1), (I2, 2), (H1, 4),),
    (HEADS, 2, 0): ((U1, 1),),
    (HEADS, 2, 2): ((H2, 3),),
    (HEADS, 3, 0): ((O, 3),),
    (HEADS, 3, 1): ((I0, 2),),
    (HEADS, 3, 2): ((U2, 1),),
    (HEADS, 3, 3): ((I1, 2), (H2, 4),),
    (PROJECT, 2): ((I2, 3),),
    (HEADS, 4, 1): ((I3, 3), (U0, 1),),
    (HEADS, 4, 2): ((I0, 3),),
    (HEADS, 5, 1): ((O, 4), (O, LOAD),),
    (HEADS, 5, 2): ((U1, 2), (I0, 4), (I0, LOAD),),
    (HEADS, 5, 3): ((I1, 3),),
    (OUT, 1): ((U0, 2),),
    (INNER, 0, 0): ((I1, 4), (I1, LOAD),),
    (INNER, 1, 0): ((U2, 2), (I2, 4), (I2, LOAD),),
    (INNER, 1, 1): ((U1, 3),),
    (INNER, 2, 0): ((U0, 3), (I3, 4), (I3, LOAD),),
    (INNER, 3, 0): ((U0, 4), (U0, LOAD),),
    (INNER, 3, 1): ((U2, 3),),
    (INNER, 3, 2): ((U1, 4), (U1, LOAD),),
    (OUTER, 0, 1): ((U2, 4), (U2, LOAD),),
}
INNER_STEPS = {
    (INNER, 1, 0): ((I0, 1),),
    (INNER, 2, 0): ((I0, 2),),
    (BACK, 2, 0): ((I1, 1),),
    (GELU, 3, 0): ((I2, 1),),
    (INNER, 3, 1): ((I0, 3),),
    (BACK, 3, 0): ((I1, 2), (I2, 2),),
    (BACK, 3, 2): ((I3, 1),),
    (NORM, 1): ((I1, 3),),
    (MIXED, 1): ((I2, 3), (I3, 2),),
    (OUTER, 0, 1): ((I0, 4), (I3, 3),),
    (OUTER, 2, 1): ((I2, 4),),
    (OUTER, 2, 3): ((I1, 4), (I3, 4),),
}
TAIL_STEPS = {
    (BEFORE, 0): ((O, 0),),
    (HEADS, 0, 0): ((U2, 0), (O, 1),),
    (HEADS, 0, 1): ((U0, 0),),
    (HEADS, 1, 0): ((U1, 0),),
    (HEADS, 1, 2): ((U2, 1),),
    (HEADS, 1, 3): ((U1, 1), (O, 2),),
    (PROJECT, 0): ((U0, 1),),
    (PROJECT, 1): ((U1, 2), (U2, 2),),
    (HEADS, 4, 0): ((H0, 1),),
    (HEADS, 4, 2): ((U1, 3),),
    (HEADS, 4, 3): ((H1, 1),),
    (HEADS, 5, 0): ((U2, 3), (O, 3), (H0, 2),),
    (HEADS, 5, 1): ((H1, 2),),
    (PROJECT, 2): ((U0, 2), (H0, 3), (H1, 3), (H2, 1),),
    (AFTER, 1): ((U0, 3), (H2, 2),),
    (AFTER, 2): ((U2, 4), (O, 4), (H0, 4), (H2, 3),),
    (AFTER, 3): ((H1, 4),),
    (AFTER, 4): ((U0, 4), (U1, 4), (H2, 4),),
}
GATHER_PARTS = {"s": ("s", (("A", 0, 128),))}
for c in range(3):
    GATHER_PARTS[f"h{c}"] = ("h", (("A", c * 256, 128), ("B", c * 256 + 128, 128)))
    GATHER_PARTS[f"u{c}"] = (
        "u",
        tuple((t, c * 256 + p * 128, 128) for p, t in enumerate(GATHER_TYPES[f"u{c}"])),
    )
for name in ("o", "i0", "i1", "i2", "i3"):
    first = int(name[1:] or 0) * D
    GATHER_PARTS[name] = (
        name[0],
        tuple((t, first + p * 256, 256) for p, t in enumerate(GATHER_TYPES[name])),
    )
GATHER_JOBS = {}
for name, (_, parts) in GATHER_PARTS.items():
    for part, (kind, _, _) in enumerate(parts):
        for s, moves in enumerate(GATHER_ORDER[kind] + (((CORE,), (CORE,)),)):
            for move in range(len(moves)):
                GATHER_JOBS[name, part, s, move] = len(GATHER_JOBS)


class Where:
    def __init__(self, lanes):
        self.dp = lax.axis_index("dp")
        self.shard = lax.axis_index("shard")
        self.lanes = lanes
        group = (self.dp * 2 + self.shard) // lanes
        self.bits = [lax.rem(group // (16 >> e), 2) for e in range(5)]

    def partner(self, *flips):
        dp, shard = self.dp, self.shard
        for e in flips:
            step = (16 >> e) * self.lanes
            if step == 1:
                shard = 1 - shard
            else:
                step = step // 2
                dp = dp + step - 2 * step * self.bits[e]
        return (dp, shard)

    def barrier(self, moves=((0,), (1,), (0, 1), (2,), (3,), (4,))):
        bar = pltpu.get_barrier_semaphore()
        for move in moves:
            pl.semaphore_signal(
                bar, inc=1, device_id=self.partner(*move), device_id_type=MESH
            )
        pl.semaphore_wait(bar, len(moves))


class Gather:
    def __init__(self, where, shards, bufs, send, recv, loc):
        self.where = where
        self.shards = shards
        self.bufs = bufs
        self.send = send
        self.recv = recv
        self.loc = loc

    def view(self, a, full, start, size, flip=()):
        index = []
        for e in range(5):
            bit = self.where.bits[e]
            index.append(slice(None) if e in full else (1 - bit if e in flip else bit))
        rest = (slice(None),) * (len(SHAPES[a]) - 1) + (pl.ds(start, size),)
        return self.bufs[a].at[tuple(index) + rest]

    def local(self, a):
        return pltpu.make_async_copy(
            self.shards[a], self.view(a, (), 0, SHAPES[a][-1]), self.loc.at[ARRAYS.index(a)]
        )

    def job(self, name, part, s, move):
        a, parts = GATHER_PARTS[name]
        kind, start, size = parts[part]
        order = GATHER_ORDER[kind]
        done = [e for stage in order[: min(s, len(order) - 1)] for m in stage for e in m]
        if s < len(order):
            flips = order[s][move]
            dst = self.view(a, done, start, size)
        else:
            flips = (CORE,)
            dst = self.view(a, done, start, size, flip=order[-1][0] if move else ())
        src = dst
        if s == 0:
            rest = (slice(None),) * (len(SHAPES[a]) - 1) + (pl.ds(start, size),)
            src = self.shards[a].at[rest]
        n = GATHER_JOBS[name, part, s, move]
        return pltpu.make_async_remote_copy(
            src_ref=src,
            dst_ref=dst,
            send_sem=self.send.at[n],
            recv_sem=self.recv.at[n],
            device_id=self.where.partner(*flips),
            device_id_type=MESH,
        )

    def step(self, name, s):
        for part, (kind, _, _) in enumerate(GATHER_PARTS[name][1]):
            order = GATHER_ORDER[kind]
            last = len(order)
            if 0 < s <= last:
                for move in range(len(order[s - 1])):
                    self.job(name, part, s - 1, move).wait_recv()
            if s < last:
                for move in range(len(order[s])):
                    self.job(name, part, s, move).start()
            if s == last - 1:
                self.job(name, part, last, 0).start()
            if s == last:
                self.job(name, part, last, 1).start()
            if s == last + 1:
                self.job(name, part, last, 0).wait_recv()
                self.job(name, part, last, 1).wait_recv()

    def drain(self):
        for key in GATHER_JOBS:
            self.job(*key).wait_send()


SCATTER_ORDER = {
    "A": (((CORE,),), ((4,),), ((2,),), LINE),
    "B": (((CORE,),), ((2,),), ((4,),), LINE),
}
INNER_PARTS = {f"i{m}{h}": (h, ROWS, 384) for m in range(4) for h in "AB"}
LATE_PARTS = {f"u{c}{h}": (h, 4 * ROWS, 128) for c in range(3) for h in "AB"}
LATE_PARTS.update({f"o{h}": (h, ROWS, 384) for h in "AB"})
HEAD_PARTS = {f"h{c}{h}": (h, 3 * ROWS + 8, 128) for c in range(3) for h in "AB"}
TAIL_PARTS = {**LATE_PARTS, **HEAD_PARTS}


def scatter_jobs(parts):
    jobs = {}
    for name, (kind, _, _) in parts.items():
        for s, moves in enumerate(SCATTER_ORDER[kind]):
            for move in range(len(moves)):
                jobs[name, s, move] = len(jobs)
    return jobs


def scatter_scratch(parts):
    scratch = []
    for _, rows, size in parts.values():
        scratch += [
            pltpu.VMEM(dims + (rows, size), BF)
            for dims in ((2,) * 5, (2,) * 4, (2,) * 3, (2,) * 2, (3,))
        ]
    jobs = len(scatter_jobs(parts))
    return scratch + [pltpu.SemaphoreType.DMA((jobs,)), pltpu.SemaphoreType.DMA((jobs,))]


def scatter_count(parts):
    return 5 * len(parts) + 2


class Scatter:
    def __init__(self, where, parts, refs):
        self.where = where
        self.parts = parts
        self.grads = {name: refs[5 * i] for i, name in enumerate(parts)}
        self.landing = {name: refs[5 * i + 1 : 5 * i + 5] for i, name in enumerate(parts)}
        self.send, self.recv = refs[5 * len(parts) :]
        self.jobs = scatter_jobs(parts)

    def index(self, name, s, flips):
        order = SCATTER_ORDER[self.parts[name][0]]
        moved = [e for stage in order[: s + 1] for m in stage for e in m]
        index = []
        for e in range(5):
            bit = self.where.bits[e]
            index.append((1 - bit if e in flips else bit) if e in moved else slice(None))
        return tuple(index)

    def job(self, name, s, move):
        flips = SCATTER_ORDER[self.parts[name][0]][s][move]
        n = self.jobs[name, s, move]
        landing = self.landing[name][s]
        return pltpu.make_async_remote_copy(
            src_ref=self.grads[name].at[self.index(name, s, flips)],
            dst_ref=landing.at[move] if s == 3 else landing,
            send_sem=self.send.at[n],
            recv_sem=self.recv.at[n],
            device_id=self.where.partner(*flips),
            device_id_type=MESH,
        )

    def add(self, name, s):
        index = self.index(name, s, ())
        grads, landing = self.grads[name], self.landing[name][s]
        if s == 3:
            total = grads[index].astype(F32)
            for move in range(3):
                total = total + landing[move].astype(F32)
            grads[index] = total.astype(BF)
            return
        free = [e for e in range(5) if isinstance(index[e], slice)]

        def one(t, _):
            bits = [lax.rem(t // (1 << (3 - s - k)), 2) for k in range(4 - s)]
            at = list(index)
            for k, e in enumerate(free):
                at[e] = bits[k]
            grads[tuple(at)] = grads[tuple(at)] + landing[tuple(bits)]
            return 0

        lax.fori_loop(0, 1 << (4 - s), one, 0)

    def step(self, name, s):
        for half in "AB":
            part = name + half
            moves = SCATTER_ORDER[half]
            if s > 0:
                for move in range(len(moves[s - 1])):
                    self.job(part, s - 1, move).wait_recv()
                self.add(part, s - 1)
            if s < 4:
                for move in range(len(moves[s])):
                    self.job(part, s, move).start()

    def own(self, part):
        return self.grads[part][tuple(self.where.bits)].astype(F32)

    def drain(self):
        for key in self.jobs:
            self.job(*key).wait_send()


def spread(dst, value, rows, at):
    dims = len(dst.shape) - 2
    for g in range(1 << dims):
        bits = tuple((g >> (dims - 1 - e)) & 1 for e in range(dims))
        dst[bits + (slice(at, at + rows),)] = value[g * rows : (g + 1) * rows].astype(BF)


def rows_of(t, size):
    return pl.ds(pl.multiple_of(t * size, size), size)


def assemble(w, staged, cols):
    for g in range(GROUPS):
        bits = tuple((g >> (4 - e)) & 1 for e in range(5))
        w[g * ROWS : (g + 1) * ROWS, cols] = staged[bits]


def fill_turn(c_ref, row_ref, transposed):
    col_ref = row_ref[...].T
    for i in range(NB):
        for j in range(NB):
            if (j < i) if transposed else (j > i):
                continue
            r, w = slice(i * B, (i + 1) * B), slice(j * B, (j + 1) * B)
            turn = col_ref[r, 0:1] * row_ref[0:1, w] + col_ref[r, 1:2] * row_ref[1:2, w]
            allowed = col_ref[r, 2:3] == row_ref[2:3, w]
            if i == j:
                mine = lax.broadcasted_iota(jnp.int32, (B, B), 0)
                other = lax.broadcasted_iota(jnp.int32, (B, B), 1)
                allowed &= (other >= mine) if transposed else (other <= mine)
            c_ref[r, w] = jnp.where(allowed, turn, 0.0).astype(BF)


def normalize(h):
    center = h - jnp.mean(h, axis=1, keepdims=True)
    rstd = lax.rsqrt(jnp.mean(center * center, axis=1, keepdims=True) + 1e-05)
    return center * rstd, rstd


KEPT = ("q", "k", "v", "o", "rd", "mixed", "hat", "rstd", "low", "inner", "wq", "wk", "wv")


def forward_kernel(lanes, *refs):
    n = len(ARRAYS)
    shards = dict(zip(ARRAYS, refs[:n]))
    x_in, row, cot_in = refs[n : n + 3]
    refs = refs[n + 3 :]
    bufs = dict(zip("oiu", refs[:3]))
    result, g_second, vec, sums = refs[3:7]
    kept_out = refs[7 : 7 + len(KEPT)]
    refs = refs[7 + len(KEPT) :]
    kept = refs[: len(KEPT)]
    q, k, v, o, rd, mixed, hat, rstd, low, inner, *heads = kept
    (
        small, all_h, staged, staged_u, w, c_ref, fq, fk0, fk1, v0, v1, acc, act,
        b_inner, send, recv, loc, load, keep_sem, x,
    ) = refs[len(KEPT) :]
    bufs["s"], bufs["h"] = small, all_h
    gather = Gather(Where(lanes), shards, bufs, send, recv, loc)
    for a in ARRAYS:
        gather.local(a).start()

    def keep(name):
        i = KEPT.index(name)
        return pltpu.make_async_copy(kept[i], kept_out[i], keep_sem.at[i])

    def loads(name):
        j = int(name[1:] or 0)
        if name[0] == "u":
            src = bufs["u"].at[(slice(None),) * 6 + (pl.ds(j * 256, 256),)]
            return [pltpu.make_async_copy(src, staged_u.at[j % 2], load.at[j % 2])]
        at = 0 if name == "o" else (j + 1) % 2
        src = bufs[name[0]].at[(slice(None),) * 6 + (pl.ds(j * D, D),)]
        return [pltpu.make_async_copy(src, staged.at[at], load.at[3 + at])]

    def slot(*place):
        for name, what in FORWARD_STEPS.get(place, ()):
            if what == LOAD:
                for copy in loads(name):
                    copy.start()
            else:
                gather.step(name, what)

    def arrived(name):
        for copy in loads(name):
            copy.wait()

    gather.where.barrier()
    slot(BEFORE, 0)
    x_copy = pltpu.make_async_copy(x_in, x, load.at[5])
    x_copy.start()
    fill_turn(c_ref, row, False)
    for a in ARRAYS:
        gather.local(a).wait()
    for i in range(1, 8):
        slot(BEFORE, i)
    vec[...] = jnp.zeros_like(vec)
    b_inner[...] = jnp.zeros_like(b_inner)
    lane = lax.broadcasted_iota(jnp.int32, (16, 256), 1)
    for g in range(GROUPS):
        bits = tuple((g >> (4 - e)) & 1 for e in range(5))
        mine = small[bits].astype(F32)
        mine = jnp.concatenate([mine, jnp.zeros_like(mine)], axis=1)
        for dst, rows, width in ((vec, slice(0, 16), ROWS), (b_inner, slice(8, 16), 4 * ROWS)):
            at = g * width
            piece = jnp.where(lane < width, mine, 0.0)
            if at % 128:
                piece = pltpu.roll(piece, at % 128, 1)
            at = at // 128 * 128
            dst[:, at : at + 256] += piece[rows]
    for c in range(3):
        cols = slice(c * 256, c * 256 + 256)
        if c == 0:
            x_copy.wait()
        for i, out in enumerate((q, k, v)):
            assemble(heads[i], all_h.at[:, :, :, :, :, i, :, cols], cols)
            out[:, cols] = (nn(x[...], heads[i][:, cols]) + vec[i : i + 1, cols]).astype(BF)
        slot(PROJECT, c)
        if c == 2:
            for name in ("q", "k", "v", "wq", "wk", "wv"):
                keep(name).start()

        def between(hp, i):
            for at in (2 * c, 2 * c + 1):
                if (HEADS, at, i) in FORWARD_STEPS:
                    pl.when(hp == at)(lambda at=at: slot(HEADS, at, i))

        attend(2 * c, c_ref, q, k, v, o, rd, fq, fk0, fk1, v0, v1, between)
    keep("o").start()
    keep("rd").start()
    arrived("o")
    assemble(w, staged.at[0], slice(0, D))

    def attended(t, _):
        r = rows_of(t, B)
        low_mixed = o[r, :].astype(BF)
        mixed[r, :] = low_mixed
        first = x[r, :].astype(F32) + nn(low_mixed, w[...]) + vec[3:4, :D]
        xhat, spread = normalize(first)
        hat[r, :] = xhat.astype(BF)
        rstd[r, :] = jnp.broadcast_to(spread, (B, 128))
        normed = xhat * vec[4:5, :D] + vec[5:6, :D]
        low[r, :] = normed.astype(BF)
        acc[r, :] = normed + vec[6:7, :D]
        return 0

    lax.fori_loop(0, 2, attended, 0)
    slot(OUT, 0)
    lax.fori_loop(2, 4, attended, 0)
    slot(OUT, 1)
    for name in ("mixed", "hat", "rstd", "low"):
        keep(name).start()
    keep("q").wait()
    cot_copy = pltpu.make_async_copy(cot_in, q, load.at[5])
    cot_copy.start()
    for j in range(4):
        arrived(f"i{j}")
        assemble(w, staged.at[(j + 1) % 2], slice(0, D))
        for n in range(3):
            cols = slice(j * D + n * 256, j * D + n * 256 + 256)
            hidden = nn(low[...], w[:, n * 256 : n * 256 + 256]) + b_inner[1:2, cols]
            inner[:, cols] = hidden.astype(BF)
            act[:, cols] = jax.nn.gelu(hidden).astype(BF)
            slot(INNER, j, n)
    keep("inner").start()
    for c in range(3):
        cols = slice(c * 256, c * 256 + 256)
        arrived(f"u{c}")
        for half in range(2):
            r = slice(half * 512, half * 512 + 512)
            acc[r, cols] += nn(act[r, :], staged_u[c % 2].reshape(FF, 256))
            slot(OUTER, c, half)
    sums[...] = jnp.zeros_like(sums)
    cot_copy.wait()

    def final(t, _):
        r = rows_of(t, 128)
        xhat, spread = normalize(acc[r, :])
        gain = vec[7:8, :D]
        result[r, :] = (xhat * gain + vec[8:9, :D]).astype(BF)
        back = q[r, :].astype(F32)
        scaled = back * gain
        g = spread * (
            scaled
            - jnp.mean(scaled, axis=1, keepdims=True)
            - xhat * jnp.mean(scaled * xhat, axis=1, keepdims=True)
        )
        g_second[r, :] = g
        sums[6:7, :] += jnp.sum(g.astype(BF).astype(F32), axis=0, keepdims=True)
        sums[7:8, :] += jnp.sum(back * xhat, axis=0, keepdims=True)
        sums[8:9, :] += jnp.sum(back, axis=0, keepdims=True)
        return 0

    lax.fori_loop(0, T // 128, final, 0)
    for name in KEPT[1:]:
        keep(name).wait()
    gather.drain()


def forward(lanes, arrays, x, row, cot):
    anywhere = pl.BlockSpec(memory_space=pl.ANY)
    vmem = pl.BlockSpec(memory_space=pltpu.VMEM)
    jobs = len(GATHER_JOBS)
    rows, wide = ((T, D), BF), ((T, D), F32)
    kept = [
        rows, rows, rows, wide, rows, rows, rows, ((T, 128), F32), rows, ((T, FF), BF),
        ((D, D), BF), ((D, D), BF), ((D, D), BF),
    ]
    outs = [((2,) * 5 + SHAPES[a], BF) for a in "oiu"]
    outs += [rows, wide, ((16, D + 128), F32), ((16, D), F32)] + kept
    return pl.pallas_call(
        lambda *refs: forward_kernel(lanes, *refs),
        out_shape=tuple(jax.ShapeDtypeStruct(*out) for out in outs),
        in_specs=[vmem] * len(ARRAYS) + [anywhere, vmem, anywhere],
        out_specs=(anywhere,) * 3 + (vmem,) * 4 + (anywhere,) * len(kept),
        scratch_shapes=[
            *[pltpu.VMEM(*one) for one in kept],
            pltpu.VMEM((2,) * 5 + SHAPES["s"], BF),
            pltpu.VMEM((2,) * 5 + SHAPES["h"], BF),
            pltpu.VMEM((2,) + (2,) * 5 + (ROWS, D), BF),
            pltpu.VMEM((2,) + (2,) * 5 + (FF // GROUPS, 256), BF),
            pltpu.VMEM((D, D), BF),
            pltpu.VMEM((T, T), BF),
            *[pltpu.VMEM((T, 128), BF)] * 5,
            pltpu.VMEM((T, D), F32),
            pltpu.VMEM((T, FF), BF),
            pltpu.VMEM((8, FF + 128), F32),
            pltpu.SemaphoreType.DMA((jobs,)),
            pltpu.SemaphoreType.DMA((jobs,)),
            pltpu.SemaphoreType.DMA((len(ARRAYS),)),
            pltpu.SemaphoreType.DMA((6,)),
            pltpu.SemaphoreType.DMA((len(kept),)),
            pltpu.VMEM((T, D), BF),
        ],
        compiler_params=pltpu.CompilerParams(
            collective_id=3, has_side_effects=True, vmem_limit_bytes=61 * MIB
        ),
        name="forward",
    )(*arrays, x, row, cot)


def attend(first, c_ref, q_ref, k_ref, v_ref, o_ref, rd_ref, fq, fk0, fk1, v0, v1, between):
    left = lax.broadcasted_iota(jnp.int32, (T, 128), 1) < 64
    left_block = lax.broadcasted_iota(jnp.int32, (B, 128), 1) < 64

    def pair(hp, _):
        sl = pl.ds(pl.multiple_of(hp * 128, 128), 128)
        fq[...] = softplus(q_ref[:, sl].astype(F32)).astype(BF)
        sk = softplus(k_ref[:, sl].astype(F32))
        fk0[...] = jnp.where(left, sk, 0.0).astype(BF)
        fk1[...] = jnp.where(left, 0.0, sk).astype(BF)
        vv = v_ref[:, sl].astype(F32)
        v0[...] = jnp.where(left, vv, 1.0).astype(BF)
        v1[...] = jnp.where(left, 1.0, vv).astype(BF)
        for i in range(NB):
            r, w = slice(i * B, (i + 1) * B), slice(0, (i + 1) * B)
            sums = []
            for fk, vx in ((fk0, v0), (fk1, v1)):
                weight = nt(fq[r], fk[w]).astype(BF) * c_ref[r, w]
                sums.append(nn(weight, vx[w]))
            numer = jnp.where(left_block, sums[0], sums[1])
            denom = pltpu.roll(jnp.where(left_block, sums[1], sums[0]), 64, 1)
            rd = 1.0 / denom
            o_ref[r, sl] = numer * rd
            rd_ref[r, sl] = rd.astype(BF)
            between(hp, i)
        return 0

    lax.fori_loop(first, first + 2, pair, 0)


def inner_back_kernel(lanes, *refs):
    given = refs[:9]
    vec, sums_in = refs[9:11]
    late_out = dict(zip(LATE_PARTS, refs[11:19]))
    g_low_out, g_mixed_out, sums, shares = refs[19:23]
    held = refs[23:32]
    gn, hid, wu, lo, wi, hat, rstd, mixed, wo = held
    act = refs[32]
    late = dict(zip(LATE_PARTS, refs[33:41]))
    gb, g_low, g_mixed, load_sem, late_sem, quarter_sem = refs[41:47]
    scatter = Scatter(Where(lanes), INNER_PARTS, refs[47:])

    def load(i):
        return pltpu.make_async_copy(given[i], held[i], load_sem.at[i])

    def keep(name):
        if name in late:
            i = list(late).index(name)
            return pltpu.make_async_copy(late[name], late_out[name], late_sem.at[i])
        src, dst, i = (g_low, g_low_out, 8) if name == "low" else (g_mixed, g_mixed_out, 9)
        return pltpu.make_async_copy(src, dst, late_sem.at[i])

    def slot(*place):
        for name, s in INNER_STEPS.get(place, ()):
            scatter.step(name, s)

    def quarter(m):
        part = pl.ds(m * D, D)
        return [
            pltpu.make_async_copy(given[2].at[part], wu.at[part], quarter_sem.at[0, m]),
            pltpu.make_async_copy(
                given[1].at[:, part], hid.at[:, part], quarter_sem.at[1, m]
            ),
        ]

    load(0).start()
    for m in range(4):
        for copy in quarter(m):
            copy.start()
        if m == 0:
            load(3).start()
            load(4).start()
    for i in range(5, 9):
        load(i).start()
    scatter.where.barrier()
    sums[...] = sums_in[...]
    load(0).wait()
    gb[...] = gn[...].astype(BF)
    c0 = math.sqrt(2.0 / math.pi)
    for m in range(4):
        for copy in quarter(m):
            copy.wait()
        for n in range(3):
            at = n * 256
            cols = slice(m * D + at, m * D + at + 256)
            back = nt(gb[...], wu[cols, :])
            h = hid[:, cols].astype(F32)
            square = h * h
            t = jnp.tanh(c0 * h * (1.0 + 0.044715 * square))
            half = 0.5 + 0.5 * t
            act[:, cols] = (h * half).astype(BF)
            slope = half + 0.5 * h * (1.0 - t * t) * (c0 * (1.0 + 3 * 0.044715 * square))
            g = (back * slope).astype(BF)
            hid[:, cols] = g
            sums[9 + m : 10 + m, at : at + 256] = jnp.sum(
                g.astype(F32), axis=0, keepdims=True
            )
            slot(GELU, m, n)
        if m == 0:
            load(3).wait()
            load(4).wait()
        for h, half in enumerate("AB"):
            cols = slice(m * D + h * 384, m * D + h * 384 + 384)
            spread(scatter.grads[f"i{m}{half}"], tn(lo[...], hid[:, cols]), ROWS, 0)
            if h:
                scatter.step(f"i{m}", 0)
            slot(INNER, m, h)
        for n in range(3):
            at = n * 256
            gn[:, at : at + 256] += nt(
                hid[:, m * D : (m + 1) * D], wi[at : at + 256, m * D : (m + 1) * D]
            )
            slot(BACK, m, n)
    for i in range(5, 9):
        load(i).wait()

    def first_back(t, _):
        r = rows_of(t, 128)
        g = gn[r, :]
        xhat = hat[r, :].astype(F32)
        sums[4:5, :] += jnp.sum(g * xhat, axis=0, keepdims=True)
        sums[5:6, :] += jnp.sum(g, axis=0, keepdims=True)
        scaled = g * vec[4:5, :D]
        g_first = rstd[r, 0:1] * (
            scaled
            - jnp.mean(scaled, axis=1, keepdims=True)
            - xhat * jnp.mean(scaled * xhat, axis=1, keepdims=True)
        )
        g_attended = g_first.astype(BF)
        g_low[r, :] = g_attended
        sums[3:4, :] += jnp.sum(g_attended.astype(F32), axis=0, keepdims=True)
        return 0

    lax.fori_loop(0, 4, first_back, 0)
    slot(NORM, 0)
    lax.fori_loop(4, 8, first_back, 0)
    slot(NORM, 1)
    keep("low").start()
    for n in range(3):
        at = n * 256
        g_mixed[:, at : at + 256] = nt(g_low[...], wo[at : at + 256, :]).astype(BF)
        slot(MIXED, n)
    keep("mixed").start()
    for h, half in enumerate("AB"):
        spread(late["o" + half], tn(mixed[...], g_low[:, h * 384 : h * 384 + 384]), ROWS, 0)
        keep("o" + half).start()
        slot(OUT, h)
    for c in range(3):
        for m in range(4):
            value = tn(act[:, m * D : (m + 1) * D], gb[:, c * 256 : c * 256 + 256])
            for h, half in enumerate("AB"):
                spread(
                    late[f"u{c}{half}"].at[m // 2, m % 2],
                    value[:, h * 128 : h * 128 + 128],
                    4 * ROWS,
                    0,
                )
            slot(OUTER, c, m)
        for half in "AB":
            keep(f"u{c}{half}").start()
    for m in range(4):
        shares[:, m * D : m * D + 384] = scatter.own(f"i{m}A")
        shares[:, m * D + 384 : (m + 1) * D] = scatter.own(f"i{m}B")
    for name in (*late, "low", "mixed"):
        keep(name).wait()
    scatter.drain()


def inner_back(lanes, given, vec, sums):
    anywhere = pl.BlockSpec(memory_space=pl.ANY)
    vmem = pl.BlockSpec(memory_space=pltpu.VMEM)
    rows = ((T, D), BF)
    late = [((2,) * 5 + p[1:], BF) for p in LATE_PARTS.values()]
    outs = late + [rows, rows, ((16, D), F32), ((ROWS, FF), F32)]
    return pl.pallas_call(
        lambda *refs: inner_back_kernel(lanes, *refs),
        out_shape=tuple(jax.ShapeDtypeStruct(*out) for out in outs),
        in_specs=[anywhere] * 9 + [vmem] * 2,
        out_specs=(anywhere,) * (len(late) + 2) + (vmem,) * 2,
        scratch_shapes=[
            *[pltpu.VMEM(g.shape, g.dtype) for g in given],
            pltpu.VMEM((T, FF), BF),
            *[pltpu.VMEM(*one) for one in late],
            *[pltpu.VMEM(*rows)] * 3,
            pltpu.SemaphoreType.DMA((9,)),
            pltpu.SemaphoreType.DMA((len(late) + 2,)),
            pltpu.SemaphoreType.DMA((2, 4)),
            *scatter_scratch(INNER_PARTS),
        ],
        compiler_params=pltpu.CompilerParams(
            collective_id=4, has_side_effects=True, vmem_limit_bytes=61 * MIB
        ),
        name="inner_back",
    )(*given, vec, sums)


def heads_back_kernel(lanes, *refs):
    late = dict(zip(LATE_PARTS, refs[:8]))
    given = refs[8:19]
    row, sums_in = refs[19:21]
    tokens_grad, share_q, share_k, share_v, share_o, share_u, total = refs[21:28]
    held = refs[28:39]
    q, k, v, o, rd, gm, x, g_low, wq, wk, wv = held
    (
        ct, gq, gk, gv, fq, fk0, fk1, v0, v1, g0, g1, e0, e1, aq,
        landing, vec_send, vec_recv, load_sem, late_sem, pair_sem, sums,
    ) = refs[39:60]
    scatter = Scatter(Where(lanes), TAIL_PARTS, refs[60:])
    sums[...] = jnp.zeros_like(sums)
    where = scatter.where

    def pair_load(i, hp):
        sl = pl.ds(pl.multiple_of(hp * 128, 128), 128)
        return pltpu.make_async_copy(
            given[i].at[:, sl], held[i].at[:, sl], pair_sem.at[i, hp]
        )

    def whole_load(i):
        return pltpu.make_async_copy(given[i], held[i], load_sem.at[i])

    def slot(*place):
        for name, s in TAIL_STEPS.get(place, ()):
            if s == 0:
                for half in "AB":
                    load(name + half).wait()
            scatter.step(name, s)

    def load(name):
        return pltpu.make_async_copy(
            late[name], scatter.grads[name], late_sem.at[list(late).index(name)]
        )

    def first_loads(hp, _):
        for i in range(6):
            pair_load(i, hp).start()
        return 0

    first_loads(0, 0)
    for name in late:
        load(name).start()
    lax.fori_loop(1, 6, first_loads, 0)
    for i in range(6, 11):
        whole_load(i).start()
    where.barrier()
    fill_turn(ct, row, True)
    slot(BEFORE, 0)
    lane = lax.broadcasted_iota(jnp.int32, (T, 128), 1)
    left = lane < 64
    left_block = lax.broadcasted_iota(jnp.int32, (B, 128), 1) < 64

    def pair(hp, _):
        for i in range(6):
            pair_load(i, hp).wait()
        sl = pl.ds(pl.multiple_of(hp * 128, 128), 128)
        fq[...] = softplus(q[:, sl].astype(F32)).astype(BF)
        sk = softplus(k[:, sl].astype(F32))
        fk0[...] = jnp.where(left, sk, 0.0).astype(BF)
        fk1[...] = jnp.where(left, 0.0, sk).astype(BF)
        vv = v[:, sl].astype(F32)
        v0[...] = jnp.where(left, vv, 1.0).astype(BF)
        v1[...] = jnp.where(left, 1.0, vv).astype(BF)
        gn = (gm[:, sl].astype(F32) * rd[:, sl]).astype(BF).astype(F32)
        through = gn * o[:, sl]
        d0 = -jnp.sum(jnp.where(left, through, 0.0), axis=1, keepdims=True)
        d1 = -jnp.sum(jnp.where(left, 0.0, through), axis=1, keepdims=True)
        h0 = d0.astype(BF).astype(F32)
        h1 = d1.astype(BF).astype(F32)
        g0[...] = jnp.where(left, gn, 0.0).astype(BF)
        g1[...] = jnp.where(left, 0.0, gn).astype(BF)
        t0 = jnp.where(lane == 64, h0, jnp.where(lane == 65, d0 - h0, 0.0))
        t1 = jnp.where(lane == 0, h1, jnp.where(lane == 1, d1 - h1, 0.0))
        e0[...] = jnp.where(left, gn, t0).astype(BF)
        e1[...] = jnp.where(left, t1, gn).astype(BF)
        aq[...] = jnp.zeros_like(aq)
        for j in range(NB):
            r, w = slice(j * B, (j + 1) * B), slice(j * B, T)
            keys, values = [], []
            for fk, vx, g, e in ((fk0, v0, g0, e0), (fk1, v1, g1, e1)):
                weight = nt(fk[r], fq[w]).astype(BF) * ct[r, w]
                change = nt(vx[r], e[w]).astype(BF) * ct[r, w]
                values.append(nn(weight, g[w]))
                keys.append(nn(change, fq[w]))
                aq[w] += tn(change, fk[r])
            gv[r, sl] = (values[0] + values[1]).astype(BF)
            back = jnp.where(left_block, keys[0], keys[1])
            gk[r, sl] = (back * jax.nn.sigmoid(k[r, sl].astype(F32))).astype(BF)
            for at in range(6):
                if (HEADS, at, j) in TAIL_STEPS:
                    pl.when(hp == at)(lambda at=at, j=j: slot(HEADS, at, j))
        gq[:, sl] = (aq[...] * jax.nn.sigmoid(q[:, sl].astype(F32))).astype(BF)
        return 0

    stages = SCATTER_ORDER["A"]

    def vector(s, move):
        n = s + move
        return pltpu.make_async_remote_copy(
            src_ref=total,
            dst_ref=landing.at[n],
            send_sem=vec_send.at[n],
            recv_sem=vec_recv.at[n],
            device_id=where.partner(*stages[s][move]),
            device_id_type=MESH,
        )

    def vectors(s):
        if s > 0:
            for move in range(len(stages[s - 1])):
                vector(s - 1, move).wait()
            for move in range(len(stages[s - 1])):
                total[...] += landing[s - 1 + move]
        if s < 4:
            for move in range(len(stages[s])):
                vector(s, move).start()

    total[...] = sums_in[...]
    vectors(0)
    for c in range(3):
        lax.fori_loop(2 * c, 2 * c + 2, pair, 0)
        cols = slice(c * 256, c * 256 + 256)
        vectors(c + 1)
        if c == 0:
            whole_load(6).wait()
        for i, g in enumerate((gq, gk, gv)):
            value = tn(x[...], g[:, cols])
            for h, half in enumerate("AB"):
                spread(
                    scatter.grads[f"h{c}{half}"],
                    value[:, h * 128 : h * 128 + 128],
                    ROWS,
                    i * ROWS,
                )
            sums[i : i + 1, cols] = jnp.sum(g[:, cols].astype(F32), axis=0, keepdims=True)
        for h, half in enumerate("AB"):
            bias_rows = sums[0:8, c * 256 + h * 128 : c * 256 + h * 128 + 128].astype(BF)
            for g in range(GROUPS):
                bits = tuple((g >> (4 - e)) & 1 for e in range(5))
                scatter.grads[f"h{c}{half}"][bits + (slice(3 * ROWS, 3 * ROWS + 8),)] = bias_rows
        scatter.step(f"h{c}", 0)
        slot(PROJECT, c)

    for i in range(7, 11):
        whole_load(i).wait()

    def tokens_part(at):
        cols = slice(at, at + 256)
        total = g_low[:, cols].astype(F32)
        for g, w in ((gq, wq), (gk, wk), (gv, wv)):
            total = total + nt(g[...], w[cols, :])
        tokens_grad[:, cols] = total.astype(BF)

    for s in range(1, 4):
        slot(AFTER, s)
        tokens_part((s - 1) * 256)
    vectors(4)
    slot(AFTER, 4)
    for c in range(3):
        for h, half in enumerate("AB"):
            cols = slice(c * 256 + h * 128, c * 256 + h * 128 + 128)
            value = scatter.own(f"h{c}{half}")
            for i, share in enumerate((share_q, share_k, share_v)):
                share[:, cols] = value[i * ROWS : (i + 1) * ROWS]
            total[0:3, cols] = value[3 * ROWS : 3 * ROWS + 3]
            share_u[:, cols] = scatter.own(f"u{c}{half}")
    for h, half in enumerate("AB"):
        share_o[:, h * 384 : h * 384 + 384] = scatter.own("o" + half)
    scatter.drain()


def heads_back(lanes, late, given, row, sums):
    anywhere = pl.BlockSpec(memory_space=pl.ANY)
    vmem = pl.BlockSpec(memory_space=pltpu.VMEM)
    shape = jax.ShapeDtypeStruct
    return pl.pallas_call(
        lambda *refs: heads_back_kernel(lanes, *refs),
        out_shape=(
            shape((T, D), BF),
            *[shape((ROWS, D), F32)] * 4,
            shape((4 * ROWS, D), F32),
            shape((16, D), F32),
        ),
        in_specs=[anywhere] * (len(late) + len(given)) + [vmem] * 2,
        out_specs=(vmem,) * 7,
        scratch_shapes=[
            *[pltpu.VMEM(g.shape, g.dtype) for g in given],
            pltpu.VMEM((T, T), BF),
            *[pltpu.VMEM((T, D), BF)] * 3,
            *[pltpu.VMEM((T, 128), BF)] * 9,
            pltpu.VMEM((T, 128), F32),
            pltpu.VMEM((6, 16, D), F32),
            pltpu.SemaphoreType.DMA((6,)),
            pltpu.SemaphoreType.DMA((6,)),
            pltpu.SemaphoreType.DMA((len(given),)),
            pltpu.SemaphoreType.DMA((len(late),)),
            pltpu.SemaphoreType.DMA((6, 6)),
            pltpu.VMEM((8, D), F32),
            *scatter_scratch(TAIL_PARTS),
        ],
        compiler_params=pltpu.CompilerParams(
            collective_id=5, has_side_effects=True, vmem_limit_bytes=61 * MIB
        ),
        name="heads_back",
    )(*late, *given, row, sums)


def hand_over(*arrays):
    def copy(*refs):
        for src, dst in zip(refs[: len(arrays)], refs[len(arrays) :]):
            dst[...] = src[...]

    vmem = pl.BlockSpec(memory_space=pltpu.VMEM)
    return pl.pallas_call(
        copy,
        out_shape=tuple(jax.ShapeDtypeStruct(a.shape, a.dtype) for a in arrays),
        in_specs=[vmem] * len(arrays),
        out_specs=(vmem,) * len(arrays),
        name="hand_over",
    )(*arrays)


def geometry(lengths, count):
    number = lengths.shape[0]
    order = jnp.arange(number, dtype=jnp.int32)
    upto = order[:, None] <= order[None, :]
    ends = jnp.sum(jnp.where(upto, lengths[:, None], 0), axis=0)
    starts = ends - lengths
    places = jnp.arange(count, dtype=jnp.int32)
    segment = jnp.sum((places[:, None] >= ends[None, :]).astype(jnp.int32), axis=1)
    onehot = segment[:, None] == order[None, :]
    begin = jnp.sum(jnp.where(onehot, starts[None, :], 0), axis=1)
    total = jnp.sum(jnp.where(onehot, lengths[None, :], 0), axis=1)
    angle = 0.5 * math.pi * (places - begin).astype(F32) / total.astype(F32)
    return segment, jnp.cos(angle), jnp.sin(angle)


def group_gather(x, lanes):
    if lanes > 1:
        x = lax.all_gather(x, "shard", axis=0, tiled=True)
    if lanes > 2:
        size = lanes // 2
        count = lax.axis_size("dp")
        parts = [list(range(i, i + size)) for i in range(0, count, size)]
        x = lax.all_gather(x, "dp", axis=0, tiled=True, axis_index_groups=parts)
    return x


def group_scatter(x, lanes):
    if lanes > 2:
        size = lanes // 2
        count = lax.axis_size("dp")
        parts = [list(range(i, i + size)) for i in range(0, count, size)]
        x = lax.psum_scatter(
            x, "dp", scatter_dimension=0, tiled=True, axis_index_groups=parts
        )
    if lanes > 1:
        x = lax.psum_scatter(x, "shard", scatter_dimension=0, tiled=True)
    return x


def body(
    lanes, tokens, seq_lengths,
    query_weight, query_bias, key_weight, key_bias, value_weight, value_bias,
    output_weight, output_bias, norm_gain, norm_shift, inner_weight, inner_bias,
    outer_weight, outer_bias, final_gain, final_shift, cotangent,
):
    segment, cosine, sine = geometry(seq_lengths[0], T)
    weights = [
        group_gather(w, lanes)
        for w in (
            query_weight, key_weight, value_weight, output_weight, inner_weight, outer_weight,
        )
    ]
    vectors = [
        group_gather(v, lanes).reshape(-1, ROWS)
        for v in (
            query_bias, key_bias, value_bias, output_bias, norm_gain, norm_shift,
            outer_bias, final_gain, final_shift,
        )
    ]
    small = jnp.pad(jnp.concatenate(vectors, axis=0), ((0, 0), (0, 128 - ROWS)))
    inside = group_gather(inner_bias, lanes).reshape(1, 4 * ROWS)
    inside = jnp.pad(inside, ((0, 6), (0, 128 - 4 * ROWS)))
    small = jnp.concatenate([small, inside], axis=0)
    place = jnp.stack([cosine, sine, segment.astype(F32)])
    row = jnp.pad(place, ((0, 5), (0, 0)))
    shards = [small, jnp.stack(weights[:3]), *weights[3:]]
    outs = forward(lanes, shards, tokens, row, cotangent)
    w_output, w_inner, w_outer = (g.reshape(-1, g.shape[-1]) for g in outs[:3])
    result, g_second, vec, sums = outs[3:7]
    query, key, value, mixed, inverse, mixed_low, hat, rstd, low, inner, *heads = outs[7:]
    *late, g_low, g_mixed, sums, share_i = inner_back(
        lanes, [g_second, inner, w_outer, low, w_inner, hat, rstd, mixed_low, w_output], vec,
        sums,
    )
    *heads, sums = heads_back(
        lanes, late, [query, key, value, mixed, inverse, g_mixed, tokens, g_low, *heads],
        row, sums,
    )
    tokens_grad, share_q, share_k, share_v, share_o, share_u, share_i, result = hand_over(
        *heads, share_i, result
    )
    group = (lax.axis_index("dp") * 2 + lax.axis_index("shard")) // lanes
    mine = lax.dynamic_slice(sums, (0, group * ROWS), (9, ROWS))
    vec = [group_scatter(mine[i], lanes) for i in range(9)]
    mine = lax.dynamic_slice(sums[9:13].reshape(FF), (group * 4 * ROWS,), (4 * ROWS,))
    inner_bias_grad = group_scatter(mine, lanes)
    mat = [
        group_scatter(s, lanes)
        for s in (share_q, share_k, share_v, share_o, share_i, share_u)
    ]
    return (
        result, tokens_grad,
        mat[0], vec[0], mat[1], vec[1], mat[2], vec[2], mat[3], vec[3],
        vec[4], vec[5], mat[4], inner_bias_grad, mat[5], vec[6], vec[7], vec[8],
    )


def solution(mesh):
    lanes = mesh.shape["dp"] * mesh.shape["shard"] // GROUPS
    rows, flat = P(AXES, None), P(AXES)
    return jax.shard_map(
        lambda *args: body(lanes, *args),
        mesh=mesh,
        in_specs=(rows, rows) + (rows, flat) * 4 + (flat, flat) + (rows, flat) * 2 + (flat, flat, rows),
        out_specs=(rows, rows) + (rows, flat) * 4 + (flat, flat) + (rows, flat) * 2 + (flat, flat),
        check_vma=False,
    )
```
